512 devices in a mesh: row: 64 (over z_lo, y, x), col: 8 (over z_hi, core).
Axes of the slice: x: 4, y: 4, z: 16 (z_hi: 4, z_lo: 4; z = z_hi * 4 + z_lo), core: 2. Of those that a mesh axis runs over, the one named last changes fastest.
Arguments:
- blocks: bfloat16 [128, 256, 256], P('col')
- position: int32 [128], replicated, may hold values from 0 to 15
- primal: bfloat16 [4096, 4096], P('row', 'col'), as said below
- dual_inverse: bfloat16 [4096, 4096], P('row', 'col')
Outputs:
- factor: float32 [128, 16], P('row')
- reduced: float32 [128, 128], P('row', 'col')
The draws below stay inside these ranges and needn't reach their ends.
Inputs may be any that keep to these rules, and one draw needn't show every extreme that they name: primal, dual_inverse and each block are exactly symmetric.
All inputs are finite; a program needn't handle non-finite values.
Results may differ from the reference program's by a relative error of at most 0.0003.
Values may be sent and summed in bfloat16 or wider, within the bound.
A program may use at most 64 MiB of HBM per device.

```python
import math
import jax
import jax.numpy as jnp
import numpy as np
from jax import lax

NMAT = 4096
BLOCK = 256
PANELS = 2
NPOS = 16
K = 128
PW = 8


def definite_matrix(base, order, shift):
    scaled = base
    product = jnp.dot(scaled, scaled.T, precision=lax.Precision.HIGHEST) / order
    eye_part = (jnp.arange(order)[:, None] == jnp.arange(order)[None, :]).astype(jnp.float32)
    return 0.5 * (product + product.T) + shift * eye_part


def iterate_matrix(key):
    base_key = jax.random.fold_in(key, 0)
    base = jax.random.normal(base_key, (NMAT, NMAT), jnp.float32)
    return definite_matrix(base, NMAT, 0.25).astype(jnp.bfloat16)


def draw_primal(key, part):
    key = jax.random.fold_in(key, 11)
    return iterate_matrix(key)


def draw_dual_inverse(key, part):
    key = jax.random.fold_in(key, 23)
    return iterate_matrix(key)


def draw_blocks(key, part):
    key = jax.random.fold_in(key, 37)
    shared_key, noise_key = jax.random.split(key)
    shared = jax.random.normal(shared_key, (BLOCK, BLOCK), jnp.float32)
    noise = jax.random.normal(noise_key, (K, BLOCK, BLOCK), jnp.float32)
    combined = shared[None, :, :] + noise
    return ((combined + jnp.swapaxes(combined, 1, 2)) * (0.7 / BLOCK)).astype(jnp.bfloat16)


def touch_ends(entries, stream_key, least, largest):
    longest = entries.shape.index(max(entries.shape))
    spots = []
    for shift in (0, 1):
        where = [jax.random.randint(jax.random.fold_in(stream_key, axis), (), 0, length) for axis, length in enumerate(entries.shape)]
        where[longest] = (where[longest] + shift) % entries.shape[longest]
        spots.append(tuple(where))
    return entries.at[spots[0]].set(least).at[spots[1]].set(largest)


def cumulative_ranks(count, skew):
    portions = [(1 << 20) // math.isqrt(grade ** skew) + 1 for grade in range(1, count + 1)]
    scale = 1 + sum(portions) // (1 << 30)
    return np.cumsum(np.array([max(1, weight // scale) for weight in portions]))


def ranked(stream_key, extent, number_of, slope):
    listing = cumulative_ranks(number_of, slope)
    pick = jax.random.randint(jax.random.fold_in(stream_key, 1), extent, 0, int(listing[number_of - 1]))
    standing = jnp.searchsorted(jnp.asarray(listing, jnp.int32), pick, side="right")
    return jax.random.permutation(jax.random.fold_in(stream_key, 2), number_of)[standing].astype(jnp.int32)


def setup_inputs(seed: int = 0) -> dict:
    arg_keys = jax.random.split(jax.random.key(seed), 5)
    blocks = draw_blocks(jax.random.fold_in(arg_keys[4], 71), 0)
    position = touch_ends(ranked(arg_keys[1], (K,), NPOS, 2), jax.random.fold_in(arg_keys[1], 3), 0, NPOS - 1).astype(jnp.int32)
    primal = draw_primal(jax.random.fold_in(arg_keys[4], 71), 0)
    dual_inverse = draw_dual_inverse(jax.random.fold_in(arg_keys[4], 71), 0)
    return {"blocks": blocks, "position": position, "primal": primal, "dual_inverse": dual_inverse}


def panel_factor(column, low_col, panel_cols):
    diagonal = column[low_col:low_col + panel_cols]
    lower = jnp.linalg.cholesky(diagonal)
    solved = lax.linalg.triangular_solve(lower, column, left_side=False, lower=True, transpose_a=True)
    before = jnp.zeros((low_col, panel_cols), jnp.float32)
    return jnp.concatenate([before, lower, solved[low_col + panel_cols:]], axis=0)

def reference(blocks, position, primal, dual_inverse):
    blocks_wide = blocks.astype(jnp.float32)
    chosen = position[None, :] == jnp.arange(NPOS, dtype=jnp.int32)[:, None]

    def schur_row(index):
        start = (position[index] * BLOCK).astype(jnp.int32)
        x_rows = lax.dynamic_slice_in_dim(primal, start, BLOCK, 0)
        w_rows = lax.dynamic_slice_in_dim(dual_inverse, start, BLOCK, 0)
        left_prod = jnp.dot(blocks[index].astype(jnp.float32), w_rows.astype(jnp.float32), preferred_element_type=jnp.float32).astype(jnp.bfloat16)
        x_split = x_rows.reshape(BLOCK, NPOS, BLOCK).astype(jnp.float32)
        l_split = left_prod.reshape(BLOCK, NPOS, BLOCK).astype(jnp.float32)
        fields = jnp.einsum('aqc,aqd->qcd', x_split, l_split).astype(jnp.bfloat16)
        products = jnp.einsum('qcd,jcd->qj', fields.astype(jnp.float32), blocks_wide)
        return jnp.sum(jnp.where(chosen, products, 0.0), axis=0)
    schur = lax.map(schur_row, jnp.arange(K, dtype=jnp.int32))
    factor_list = []
    for panel in range(PANELS):
        low_col = panel * PW
        factor_part = panel_factor(schur[:, low_col:low_col + PW], low_col, PW)
        schur = schur - jnp.dot(factor_part, factor_part.T, precision=lax.Precision.HIGHEST)
        factor_list.append(factor_part)
    keeper = jnp.arange(K) >= PANELS * PW
    reduced = jnp.where(keeper[:, None] & keeper[None, :], schur, 0.0)
    return (jnp.concatenate(factor_list, axis=1), reduced)
```

```python
import functools

import jax
import jax.numpy as jnp
from jax import lax
from jax.experimental import pallas as pl
from jax.experimental.pallas import tpu as pltpu
from jax.sharding import PartitionSpec as P

BLOCK = 256
PANELS = 2
MESH = pl.DeviceIdType.MESH
PIECES = 2
ROWS = 8 // PIECES


def remote(src, dst, send, recv, dev):
    return pltpu.make_async_remote_copy(
        src_ref=src, dst_ref=dst, send_sem=send, recv_sem=recv, device_id=dev, device_id_type=MESH
    )


def await_bytes(ref, sem):
    pltpu.make_async_copy(ref, ref, sem).wait()


def schur_kernel(
    gt, xt, w4, pos_i, pos_j,
    factor_ref, schur_ref,
    ga, gd, xp, wp, lbuf, rbuf, acc, part, share, rs, zs,
    loc_sem, x_send, x_recv, w_send, w_recv, zr_send, zr_recv, zl_send, zl_recv,
    ya_send, xd_send, ya_recv, xd_recv, cp_sem, sa_send, sd_send, sa_recv, sd_recv, red_send, red_recv,
):
    row = lax.axis_index("row")
    col = lax.axis_index("col")
    zlo, y, x = row // 16, (row // 4) % 4, row % 4
    zhi, core = col // 2, col % 2
    z = zhi * 4 + zlo
    sibling = (row, zhi * 2 + (1 - core))

    def at_z(zz, kk):
        zz = zz % 16
        return ((zz % 4) * 16 + y * 4 + x, (zz // 4) * 2 + kk)

    def at_xy(xx, yy, kk):
        return (zlo * 16 + (yy % 4) * 4 + xx % 4, zhi * 2 + kk)

    def in_plane(m):
        return (x + m % 4) % 4, (y + m // 4) % 4

    barrier = pltpu.get_barrier_semaphore()

    def greet(dev):
        pl.semaphore_signal(barrier, inc=1, device_id=dev, device_id_type=MESH)

    for m in range(1, 16):
        xx, yy = in_plane(m)
        greet(at_xy(xx, yy, core))
        greet(at_xy(xx, yy, 1 - core))
        greet(at_z(z + m, core))
    greet(sibling)
    pl.semaphore_wait(barrier, 46)

    def cols(h):
        return pl.ds(((h % 4) * 2 + core) * 16, 16)

    right, left = at_z(z + 1, core), at_z(z + 15, core)

    def right_rows(idx):
        return (idx % (2 * PIECES)) * ROWS

    def left_rows(idx):
        return ((idx + PIECES) % (2 * PIECES)) * ROWS

    base = 64 * x + 16 * y

    @pl.when(zlo == 3)
    def _():
        for idx in range(2 * PIECES):
            t = right_rows(idx)
            remote(gt.at[pl.ds(base + t, ROWS)], ga.at[pl.ds(16 * y + t, ROWS), cols(zhi)],
                   zr_send, zr_recv.at[idx], right).start()

    @pl.when(zlo == 0)
    def _():
        for idx in range(2 * PIECES):
            t = left_rows(idx)
            remote(gt.at[pl.ds(base + t, ROWS)], ga.at[pl.ds(16 * y + t, ROWS), cols(zhi)],
                   zl_send, zl_recv.at[idx], left).start()

    for m in range(1, 4):
        remote(xt, xp.at[y], x_send, x_recv, at_xy(x, y + m, core)).start()
    for m in range(1, 16):
        xx, yy = in_plane(m)
        remote(w4.at[yy], wp.at[y * 4 + x], w_send, w_recv, at_xy(xx, yy, core)).start()
    pltpu.make_async_copy(xt, xp.at[y], loc_sem.at[0]).start()
    pltpu.make_async_copy(w4.at[y], wp.at[y * 4 + x], loc_sem.at[1]).start()

    own_a = gt.at[pl.ds(64 * x, 64)]
    pltpu.make_async_copy(own_a, ga.at[:, cols(zhi)], loc_sem.at[2]).start()
    remote(own_a, ga.at[:, cols(zhi)], sa_send.at[3], sa_recv.at[3], sibling).start()
    for s in range(4):
        own_d = gt.at[pl.ds(64 * s + 16 * y, 16)]
        pltpu.make_async_copy(own_d, gd.at[pl.ds(16 * s, 16), cols(zhi)], loc_sem.at[3]).start()
        remote(own_d, gd.at[pl.ds(16 * s, 16), cols(zhi)], sd_send.at[3], sd_recv.at[3], sibling).start()

    def spread(t, h, item):
        a_part = ga.at[pl.ds(16 * y + t, ROWS), cols(h)]
        d_part = gd.at[pl.ds(16 * x + t, ROWS), cols(h)]
        for m in range(1, 4):
            remote(a_part, a_part, ya_send.at[item], ya_recv.at[item], at_xy(x, y + m, core)).start()
            remote(a_part, d_part, xd_send.at[item], xd_recv.at[item], at_xy(x + m, y, core)).start()
        pltpu.make_async_copy(a_part, d_part, cp_sem.at[item]).start()

    def hand_over(h, item):
        await_bytes(ga.at[pl.ds(0, 48), pl.ds(0, 16)], ya_recv.at[item])
        part_a = ga.at[:, cols(h)]
        remote(part_a, part_a, sa_send.at[item], sa_recv.at[item], sibling).start()
        await_bytes(ga.at[pl.ds(0, 48), pl.ds(0, 16)], xd_recv.at[item])
        await_bytes(ga.at[pl.ds(0, 16), pl.ds(0, 16)], cp_sem.at[item])
        part_d = gd.at[:, cols(h)]
        remote(part_d, part_d, sd_send.at[item], sd_recv.at[item], sibling).start()

    for idx in range(3 * PIECES):
        first = idx < 2 * PIECES
        h = zhi + 3 if first else zhi + 2
        t = right_rows(idx)
        a_part = ga.at[pl.ds(16 * y + t, ROWS), cols(h)]
        await_bytes(a_part, zr_recv.at[idx])

        @pl.when(zlo < 3)
        def _():
            remote(a_part, a_part, zr_send, zr_recv.at[idx], right).start()

        if idx < PIECES:
            @pl.when(zlo == 3)
            def _():
                remote(a_part, a_part, zr_send, zr_recv.at[idx + 2 * PIECES], right).start()

        h2 = zhi + 1 if first else zhi + 2
        t2 = left_rows(idx)
        b_part = ga.at[pl.ds(16 * y + t2, ROWS), cols(h2)]
        await_bytes(b_part, zl_recv.at[idx])

        @pl.when(zlo > 0)
        def _():
            remote(b_part, b_part, zl_send, zl_recv.at[idx], left).start()

        if idx < PIECES:
            @pl.when(zlo == 0)
            def _():
                remote(b_part, b_part, zl_send, zl_recv.at[idx + 2 * PIECES], left).start()

        spread(t, h, 0 if first else 2)
        spread(t2, h2, 1 if first else 2)

    hand_over(zhi + 3, 0)
    hand_over(zhi + 1, 1)
    hand_over(zhi + 2, 2)

    pltpu.make_async_copy(xt, xp.at[y], loc_sem.at[0]).wait()
    pltpu.make_async_copy(w4.at[y], wp.at[y * 4 + x], loc_sem.at[1]).wait()
    pltpu.make_async_copy(own_a, ga.at[:, cols(zhi)], loc_sem.at[2]).wait()
    await_bytes(gd.at[:, pl.ds(0, 16)], loc_sem.at[3])
    await_bytes(xp.at[pl.ds(0, 3)], x_recv)
    await_bytes(wp.at[pl.ds(0, 15)], w_recv)
    for item in range(4):
        await_bytes(ga.at[:, pl.ds(0, 16)], sa_recv.at[item])
        await_bytes(gd.at[:, pl.ds(0, 16)], sd_recv.at[item])

    weights = jnp.concatenate(
        [wp[4 * p : 4 * p + 4].reshape(BLOCK, 128) for p in range(4)], axis=1
    )
    at_p = [pos_i[...] == 4 * zlo + p for p in range(4)]

    def pick(values, copies):
        total = None
        for p in range(4):
            mask = jnp.concatenate([at_p[p]] * copies, axis=0) if copies > 1 else at_p[p]
            term = jnp.where(mask, values[:, 128 * p : 128 * p + 128], 0.0)
            total = term if total is None else total + term
        return total

    @pl.loop(0, 64, step=4)
    def _(a):
        g = ga[pl.ds(a, 4)].reshape(512, BLOCK)
        full = jnp.dot(g, weights, preferred_element_type=jnp.float32)
        for s in range(4):
            lbuf[a + s] = pick(full[128 * s : 128 * s + 128], 1).astype(jnp.bfloat16)

    xq = [xp[:, :, BLOCK * q : BLOCK * q + BLOCK].reshape(256, BLOCK) for q in range(2)]
    at_q = [pos_j[...] == 2 * col + q for q in range(2)]

    @pl.loop(0, 64, step=2)
    def _(d):
        g = gd[pl.ds(d, 2)].reshape(256, BLOCK)
        for q in range(2):
            full = lax.dot_general(
                xq[q], g, (((1,), (1,)), ((), ())), preferred_element_type=jnp.float32
            )
            for s in range(2):
                start = pl.multiple_of((q * 64 + d + s) * 256, 256)
                rbuf[pl.ds(start, 256)] = jnp.where(at_q[q], full[:, 128 * s : 128 * s + 128], 0.0)

    acc[...] = jnp.zeros_like(acc)

    @pl.loop(0, 64, step=2)
    def _(a):
        lcat = jnp.concatenate([lbuf[a], lbuf[a + 1]], axis=1)
        rows = []
        for s in range(2):
            for q in range(2):
                rows.append(jnp.concatenate(
                    [rbuf[pl.ds(q * 64 * 256 + p * 64 + a + s, 64, stride=256)] for p in range(4)],
                    axis=1,
                ))
        rcat = jnp.concatenate(rows, axis=0).astype(jnp.bfloat16)
        acc[...] += jnp.dot(lcat, rcat, preferred_element_type=jnp.float32)

    part[...] = pick(acc[...], 1)

    me = y * 4 + x
    mine = pl.ds(pl.multiple_of(8 * me, 8), 8)
    for m in range(16):
        xx, yy = in_plane(m)
        theirs = part.at[pl.ds(8 * (yy * 4 + xx), 8)]
        if m:
            remote(theirs, rs.at[core * 16 + me], red_send.at[0], red_recv.at[0], at_xy(xx, yy, core)).start()
        remote(theirs, rs.at[core * 16 + me], red_send.at[0], red_recv.at[0], at_xy(xx, yy, 1 - core)).start()
    rs[core * 16 + me] = part[mine]
    await_bytes(rs.at[pl.ds(0, 31)], red_recv.at[0])
    share[...] = jnp.sum(rs[...], axis=0)
    for m in range(1, 16):
        remote(share, zs.at[z], red_send.at[1], red_recv.at[1], at_z(z + m, core)).start()
    zs[z] = share[...]
    await_bytes(zs.at[pl.ds(0, 15)], red_recv.at[1])
    await_bytes(rs.at[pl.ds(0, 31)], red_send.at[0])
    await_bytes(zs.at[pl.ds(0, 15)], red_send.at[1])
    share[...] = jnp.sum(zs[...], axis=0)
    whole = acc.at[:, pl.ds(0, 128)]
    for m in range(1, 16):
        xx, yy = in_plane(m)
        remote(share, whole.at[mine], red_send.at[2], red_recv.at[2], at_xy(xx, yy, core)).start()
    whole[mine] = share[...]
    await_bytes(zs.at[pl.ds(0, 15)], red_recv.at[2])
    await_bytes(zs.at[pl.ds(0, 15)], red_send.at[2])

    rows = lax.broadcasted_iota(jnp.int32, (128, 128), 0)
    lanes = lax.broadcasted_iota(jnp.int32, (128, 128), 1)
    schur = whole[...]
    factor = jnp.zeros((128, 128), jnp.float32)
    width = 8
    for k in range(PANELS * width):
        lo = k // width * width
        if k == lo:
            inside = (rows >= lo) & (rows < lo + width) & (lanes >= lo) & (lanes < lo + width)
            schur = jnp.where(inside, 0.5 * (schur + schur.T), schur)
        column = jnp.sum(jnp.where(lanes == k, schur, 0.0), axis=1, keepdims=True)
        pivot = jnp.sum(jnp.where(rows[:, :1] == k, column, 0.0), axis=0, keepdims=True)
        column = jnp.where(rows[:, :1] >= k, column / jnp.sqrt(pivot), 0.0)
        line = jnp.sum(jnp.where(rows == lanes, column, 0.0), axis=0, keepdims=True)
        schur = schur - column * line
        factor = jnp.where(lanes == k, column, factor)
    factor_ref[...] = factor
    bound = PANELS * width
    schur_ref[...] = jnp.where((rows >= bound) & (lanes >= bound), schur, 0.0)

    await_bytes(xp.at[pl.ds(0, 3)], x_send)
    await_bytes(wp.at[pl.ds(0, 15)], w_send)
    z_bytes = ga.at[pl.ds(0, 3 * PIECES * ROWS), pl.ds(0, 16)]
    await_bytes(z_bytes, zr_send)
    await_bytes(z_bytes, zl_send)
    for item in range(3):
        await_bytes(ga.at[pl.ds(0, 48), pl.ds(0, 16)], ya_send.at[item])
        await_bytes(ga.at[pl.ds(0, 48), pl.ds(0, 16)], xd_send.at[item])
    for item in range(4):
        await_bytes(ga.at[:, pl.ds(0, 16)], sa_send.at[item])
        await_bytes(gd.at[:, pl.ds(0, 16)], sd_send.at[item])


def on_device(blocks, position, primal, dual_inverse):
    tile_cols = blocks.shape[0]
    rows, width = primal.shape
    row_id = lax.axis_index("row")
    col_id = lax.axis_index("col")
    per_row = tile_cols * lax.axis_size("col") // lax.axis_size("row")
    count = position.shape[0]
    gt = jnp.swapaxes(blocks, 0, 1)
    w4 = dual_inverse.reshape(rows, 2, 4, 4, 16).transpose(3, 0, 1, 2, 4).reshape(4, rows, 128)
    vmem = pl.BlockSpec(memory_space=pltpu.VMEM)
    hbm = pl.BlockSpec(memory_space=pl.ANY)
    bf, f32 = jnp.bfloat16, jnp.float32
    dma = pltpu.SemaphoreType.DMA
    square = jax.ShapeDtypeStruct((count, count), f32)
    factor, schur = pl.pallas_call(
        schur_kernel,
        out_shape=(square, square),
        in_specs=[hbm, vmem, vmem, vmem, vmem],
        out_specs=(vmem, vmem),
        scratch_shapes=[
            pltpu.VMEM((64, count, BLOCK), bf),
            pltpu.VMEM((64, count, BLOCK), bf),
            pltpu.VMEM((4, rows, width), bf),
            pltpu.VMEM((16, rows, 128), bf),
            pltpu.VMEM((64, count, 128), bf),
            pltpu.VMEM((2 * 64 * 256, 128), f32),
            pltpu.VMEM((count, 512), f32),
            pltpu.VMEM((count, count), f32),
            pltpu.VMEM((8, count), f32),
            pltpu.VMEM((32, 8, count), f32),
            pltpu.VMEM((16, 8, count), f32),
            dma((4,)), dma, dma, dma, dma,
            dma, dma((3 * PIECES,)), dma, dma((3 * PIECES,)),
            dma((3,)), dma((3,)), dma((3,)), dma((3,)), dma((3,)), dma((4,)), dma((4,)), dma((4,)), dma((4,)), dma((3,)), dma((3,)),
        ],
        compiler_params=pltpu.CompilerParams(
            collective_id=0, has_side_effects=True, vmem_limit_bytes=56 << 20
        ),
        name="schur",
    )(gt, primal, w4, position.reshape(count, 1), position.reshape(1, count))
    factor_rows = lax.dynamic_slice(factor, (row_id * per_row, 0), (per_row, PANELS * 8))
    reduced = lax.dynamic_slice(schur, (row_id * per_row, col_id * tile_cols), (per_row, tile_cols))
    return factor_rows, reduced


def solution(mesh):
    in_specs = (P("col", None, None), P(), P("row", "col"), P("row", "col"))
    out_specs = (P("row", None), P("row", "col"))
    return jax.shard_map(
        on_device, mesh=mesh, in_specs=in_specs, out_specs=out_specs, check_vma=False
    )
```

```python
import functools

import jax
import jax.numpy as jnp
from jax import lax
from jax.experimental import pallas as pl
from jax.experimental.pallas import tpu as pltpu
from jax.sharding import PartitionSpec as P

BLOCK = 256
PANELS = 2
MESH = pl.DeviceIdType.MESH
ITEMS = (1, 3, 2)
PITCH = 264


def remote(src, dst, send, recv, dev):
    return pltpu.make_async_remote_copy(
        src_ref=src, dst_ref=dst, send_sem=send, recv_sem=recv, device_id=dev, device_id_type=MESH
    )


def await_bytes(ref, sem):
    pltpu.make_async_copy(ref, ref, sem).wait()


def schur_kernel(
    gt, xt, w4, pos_i, pos_j,
    factor_ref, schur_ref,
    ga, gd, xp, wp, lbuf, rbuf, acc, part, share, rs, zs,
    loc_sem, x_send, x_recv, w_send, w_recv, z_send, z_recv, v_send, v_recv,
    ya_send, xd_send, ya_recv, xd_recv, cp_sem, sa_send, sd_send, sa_recv, sd_recv, red_send, red_recv,
):
    row = lax.axis_index("row")
    col = lax.axis_index("col")
    zlo, y, x = row // 16, (row // 4) % 4, row % 4
    zhi, core = col // 2, col % 2
    z = zhi * 4 + zlo
    sibling = (row, zhi * 2 + (1 - core))

    def at_z(zz, kk):
        zz = zz % 16
        return ((zz % 4) * 16 + y * 4 + x, (zz // 4) * 2 + kk)

    def at_xy(xx, yy, kk):
        return (zlo * 16 + (yy % 4) * 4 + xx % 4, zhi * 2 + kk)

    def in_plane(m):
        return (x + m % 4) % 4, (y + m // 4) % 4

    barrier = pltpu.get_barrier_semaphore()

    def greet(dev):
        pl.semaphore_signal(barrier, inc=1, device_id=dev, device_id_type=MESH)

    for m in range(1, 16):
        xx, yy = in_plane(m)
        greet(at_xy(xx, yy, core))
        greet(at_xy(xx, yy, 1 - core))
        greet(at_z(z + m, core))
    greet(sibling)
    pl.semaphore_wait(barrier, 46)

    def cols(h):
        return pl.ds(((h % 4) * 2 + core) * 16, 16)

    base = 64 * x + 16 * y
    quarter = 4 * zlo

    def share_rows(t, h):
        return (
            ga.at[pl.ds(16 * y + t, 4), cols(h)],
            gd.at[pl.ds(16 * x + t, 4), cols(h)],
        )

    for item in ITEMS:
        remote(gt.at[pl.ds(base + quarter, 4)], ga.at[pl.ds(16 * y + quarter, 4), cols(zhi)],
               z_send.at[item], z_recv.at[item], at_z(z + 4 * item, core)).start()

    for m in range(1, 4):
        remote(xt, xp.at[y], x_send, x_recv, at_xy(x, y + m, core)).start()
    for m in range(1, 16):
        xx, yy = in_plane(m)
        remote(w4.at[yy], wp.at[y * 4 + x], w_send, w_recv, at_xy(xx, yy, core)).start()
    pltpu.make_async_copy(xt, xp.at[y], loc_sem.at[0]).start()
    pltpu.make_async_copy(w4.at[y], wp.at[y * 4 + x], loc_sem.at[1]).start()

    own_a = gt.at[pl.ds(64 * x, 64)]
    pltpu.make_async_copy(own_a, ga.at[:, cols(zhi)], loc_sem.at[2]).start()
    remote(own_a, ga.at[:, cols(zhi)], sa_send.at[0], sa_recv.at[0], sibling).start()
    for s in range(4):
        own_d = gt.at[pl.ds(64 * s + 16 * y, 16)]
        pltpu.make_async_copy(own_d, gd.at[pl.ds(16 * s, 16), cols(zhi)], loc_sem.at[3]).start()
        remote(own_d, gd.at[pl.ds(16 * s, 16), cols(zhi)], sd_send.at[0], sd_recv.at[0], sibling).start()

    def spread(t, item):
        a_part, d_part = share_rows(t, zhi + 4 - item)
        for m in range(1, 4):
            remote(a_part, a_part, ya_send.at[item], ya_recv.at[item], at_xy(x, y + m, core)).start()
            remote(a_part, d_part, xd_send.at[item], xd_recv.at[item], at_xy(x + m, y, core)).start()
        pltpu.make_async_copy(a_part, d_part, cp_sem.at[item]).start()

    def hand_over(item):
        await_bytes(ga.at[pl.ds(0, 48), pl.ds(0, 16)], ya_recv.at[item])
        part_a = ga.at[:, cols(zhi + 4 - item)]
        remote(part_a, part_a, sa_send.at[item], sa_recv.at[item], sibling).start()
        await_bytes(ga.at[pl.ds(0, 48), pl.ds(0, 16)], xd_recv.at[item])
        await_bytes(ga.at[pl.ds(0, 16), pl.ds(0, 16)], cp_sem.at[item])
        part_d = gd.at[:, cols(zhi + 4 - item)]
        remote(part_d, part_d, sd_send.at[item], sd_recv.at[item], sibling).start()

    for item in ITEMS:
        a_part, _ = share_rows(quarter, zhi + 4 - item)
        await_bytes(a_part, z_recv.at[item])
        for m in range(1, 4):
            plane = zhi * 4 + (zlo + m) % 4
            remote(a_part, a_part, v_send.at[item], v_recv.at[item, m], at_z(plane, core)).start()
        spread(quarter, item)
    for item in ITEMS:
        for m in range(1, 4):
            t = 4 * ((zlo + 4 - m) % 4)
            await_bytes(share_rows(t, zhi)[0], v_recv.at[item, m])
            spread(t, item)
    for item in ITEMS:
        hand_over(item)

    pltpu.make_async_copy(xt, xp.at[y], loc_sem.at[0]).wait()
    pltpu.make_async_copy(w4.at[y], wp.at[y * 4 + x], loc_sem.at[1]).wait()
    pltpu.make_async_copy(own_a, ga.at[:, cols(zhi)], loc_sem.at[2]).wait()
    await_bytes(gd.at[:, pl.ds(0, 16)], loc_sem.at[3])
    await_bytes(xp.at[pl.ds(0, 3)], x_recv)
    await_bytes(wp.at[pl.ds(0, 15)], w_recv)
    for item in range(4):
        await_bytes(ga.at[:, pl.ds(0, 16)], sa_recv.at[item])
        await_bytes(gd.at[:, pl.ds(0, 16)], sd_recv.at[item])

    weights = jnp.concatenate(
        [wp[4 * p : 4 * p + 4].reshape(BLOCK, 128) for p in range(4)], axis=1
    )
    at_p = [pos_i[...] == 4 * zlo + p for p in range(4)]

    def pick(values, copies):
        total = None
        for p in range(4):
            mask = jnp.concatenate([at_p[p]] * copies, axis=0) if copies > 1 else at_p[p]
            term = jnp.where(mask, values[:, 128 * p : 128 * p + 128], 0.0)
            total = term if total is None else total + term
        return total

    @pl.loop(0, 64, step=4)
    def _(a):
        g = ga[pl.ds(a, 4)].reshape(512, BLOCK)
        full = jnp.dot(g, weights, preferred_element_type=jnp.float32)
        for s in range(4):
            lbuf[a + s] = pick(full[128 * s : 128 * s + 128], 1).astype(jnp.bfloat16)

    xq = [xp[:, :, BLOCK * q : BLOCK * q + BLOCK].reshape(256, BLOCK) for q in range(2)]
    at_q = [pos_j[...] == 2 * col + q for q in range(2)]

    @pl.loop(0, 64, step=2)
    def _(d):
        g = gd[pl.ds(d, 2)].reshape(256, BLOCK)
        for q in range(2):
            full = lax.dot_general(
                xq[q], g, (((1,), (1,)), ((), ())), preferred_element_type=jnp.float32
            )
            for s in range(2):
                start = pl.multiple_of((q * 64 + d + s) * PITCH, 8)
                rbuf[pl.ds(start, 256)] = jnp.where(at_q[q], full[:, 128 * s : 128 * s + 128], 0.0)

    acc[...] = jnp.zeros_like(acc)

    @pl.loop(0, 64, step=4)
    def _(a):
        lcat = jnp.concatenate([lbuf[a + s] for s in range(4)], axis=1)
        rows = []
        for s in range(4):
            for q in range(2):
                rows.append(jnp.concatenate(
                    [rbuf[pl.ds(q * 64 * PITCH + p * 64 + a + s, 64, stride=PITCH)] for p in range(4)],
                    axis=1,
                ).astype(jnp.bfloat16))
        rcat = jnp.concatenate(rows, axis=0)
        acc[...] += jnp.dot(lcat, rcat, preferred_element_type=jnp.float32)

    part[...] = pick(acc[...], 1)

    me = y * 4 + x
    mine = pl.ds(pl.multiple_of(8 * me, 8), 8)
    for m in range(16):
        xx, yy = in_plane(m)
        theirs = part.at[pl.ds(8 * (yy * 4 + xx), 8)]
        if m:
            remote(theirs, rs.at[core * 16 + me], red_send.at[0], red_recv.at[0], at_xy(xx, yy, core)).start()
        remote(theirs, rs.at[core * 16 + me], red_send.at[0], red_recv.at[0], at_xy(xx, yy, 1 - core)).start()
    rs[core * 16 + me] = part[mine]
    await_bytes(rs.at[pl.ds(0, 31)], red_recv.at[0])
    share[...] = jnp.sum(rs[...], axis=0)
    for m in range(1, 16):
        remote(share, zs.at[z], red_send.at[1], red_recv.at[1], at_z(z + m, core)).start()
    zs[z] = share[...]
    await_bytes(zs.at[pl.ds(0, 15)], red_recv.at[1])
    await_bytes(rs.at[pl.ds(0, 31)], red_send.at[0])
    await_bytes(zs.at[pl.ds(0, 15)], red_send.at[1])
    share[...] = jnp.sum(zs[...], axis=0)
    whole = acc.at[:, pl.ds(0, 128)]
    for m in range(1, 16):
        xx, yy = in_plane(m)
        remote(share, whole.at[mine], red_send.at[2], red_recv.at[2], at_xy(xx, yy, core)).start()
    whole[mine] = share[...]
    await_bytes(zs.at[pl.ds(0, 15)], red_recv.at[2])
    await_bytes(zs.at[pl.ds(0, 15)], red_send.at[2])

    rows = lax.broadcasted_iota(jnp.int32, (128, 128), 0)
    lanes = lax.broadcasted_iota(jnp.int32, (128, 128), 1)
    schur = whole[...]
    factor = jnp.zeros((128, 128), jnp.float32)
    width = 8
    for k in range(PANELS * width):
        lo = k // width * width
        if k == lo:
            inside = (rows >= lo) & (rows < lo + width) & (lanes >= lo) & (lanes < lo + width)
            schur = jnp.where(inside, 0.5 * (schur + schur.T), schur)
        column = jnp.sum(jnp.where(lanes == k, schur, 0.0), axis=1, keepdims=True)
        pivot = jnp.sum(jnp.where(rows[:, :1] == k, column, 0.0), axis=0, keepdims=True)
        column = jnp.where(rows[:, :1] >= k, column / jnp.sqrt(pivot), 0.0)
        line = jnp.sum(jnp.where(rows == lanes, column, 0.0), axis=0, keepdims=True)
        schur = schur - column * line
        factor = jnp.where(lanes == k, column, factor)
    factor_ref[...] = factor
    bound = PANELS * width
    schur_ref[...] = jnp.where((rows >= bound) & (lanes >= bound), schur, 0.0)

    await_bytes(xp.at[pl.ds(0, 3)], x_send)
    await_bytes(wp.at[pl.ds(0, 15)], w_send)
    for item in ITEMS:
        await_bytes(ga.at[pl.ds(0, 4), pl.ds(0, 16)], z_send.at[item])
        await_bytes(ga.at[pl.ds(0, 12), pl.ds(0, 16)], v_send.at[item])
        await_bytes(ga.at[pl.ds(0, 48), pl.ds(0, 16)], ya_send.at[item])
        await_bytes(ga.at[pl.ds(0, 48), pl.ds(0, 16)], xd_send.at[item])
    for item in range(4):
        await_bytes(ga.at[:, pl.ds(0, 16)], sa_send.at[item])
        await_bytes(gd.at[:, pl.ds(0, 16)], sd_send.at[item])


def on_device(blocks, position, primal, dual_inverse):
    tile_cols = blocks.shape[0]
    rows, width = primal.shape
    row_id = lax.axis_index("row")
    col_id = lax.axis_index("col")
    per_row = tile_cols * lax.axis_size("col") // lax.axis_size("row")
    count = position.shape[0]
    gt = jnp.swapaxes(blocks, 0, 1)
    w4 = dual_inverse.reshape(rows, 2, 4, 4, 16).transpose(3, 0, 1, 2, 4).reshape(4, rows, 128)
    vmem = pl.BlockSpec(memory_space=pltpu.VMEM)
    hbm = pl.BlockSpec(memory_space=pl.ANY)
    bf, f32 = jnp.bfloat16, jnp.float32
    dma = pltpu.SemaphoreType.DMA
    square = jax.ShapeDtypeStruct((count, count), f32)
    factor, schur = pl.pallas_call(
        schur_kernel,
        out_shape=(square, square),
        in_specs=[hbm, vmem, vmem, vmem, vmem],
        out_specs=(vmem, vmem),
        scratch_shapes=[
            pltpu.VMEM((64, count, BLOCK), bf),
            pltpu.VMEM((64, count, BLOCK), bf),
            pltpu.VMEM((4, rows, width), bf),
            pltpu.VMEM((16, rows, 128), bf),
            pltpu.VMEM((64, count, 128), bf),
            pltpu.VMEM((2 * 64 * PITCH, 128), f32),
            pltpu.VMEM((count, 512), f32),
            pltpu.VMEM((count, count), f32),
            pltpu.VMEM((8, count), f32),
            pltpu.VMEM((32, 8, count), f32),
            pltpu.VMEM((16, 8, count), f32),
            dma((4,)), dma, dma, dma, dma,
            dma((4,)), dma((4,)), dma((4,)), dma((4, 4)),
            dma((4,)), dma((4,)), dma((4,)), dma((4,)), dma((4,)), dma((4,)), dma((4,)), dma((4,)), dma((4,)), dma((3,)), dma((3,)),
        ],
        compiler_params=pltpu.CompilerParams(
            collective_id=0, has_side_effects=True, vmem_limit_bytes=56 << 20
        ),
        name="schur",
    )(gt, primal, w4, position.reshape(count, 1), position.reshape(1, count))
    factor_rows = lax.dynamic_slice(factor, (row_id * per_row, 0), (per_row, PANELS * 8))
    reduced = lax.dynamic_slice(schur, (row_id * per_row, col_id * tile_cols), (per_row, tile_cols))
    return factor_rows, reduced


def solution(mesh):
    in_specs = (P("col", None, None), P(), P("row", "col"), P("row", "col"))
    out_specs = (P("row", None), P("row", "col"))
    return jax.shard_map(
        on_device, mesh=mesh, in_specs=in_specs, out_specs=out_specs, check_vma=False
    )
```

```python
import functools

import jax
import jax.numpy as jnp
from jax import lax
from jax.experimental import pallas as pl
from jax.experimental.pallas import tpu as pltpu
from jax.sharding import PartitionSpec as P

BLOCK = 256
PANELS = 2
MESH = pl.DeviceIdType.MESH
ITEMS = (1, 3, 2)
PITCH = 136


def remote(src, dst, send, recv, dev):
    return pltpu.make_async_remote_copy(
        src_ref=src, dst_ref=dst, send_sem=send, recv_sem=recv, device_id=dev, device_id_type=MESH
    )


def await_bytes(ref, sem):
    pltpu.make_async_copy(ref, ref, sem).wait()


def schur_kernel(
    blocks, xt, wt, pos,
    factor_ref, reduced_ref,
    raw, wide, w4, ga, gd, xp, wp, xw, ww, own_q, rbuf, lbuf, acc, part, share, rs, zs,
    loc_sem, x_send, x_recv, w_send, w_recv, z_send, z_recv, v_send, v_recv,
    ya_send, xd_send, ya_recv, xd_recv, cp_sem, sa_send, sd_send, sa_recv, sd_recv, red_send, red_recv,
):
    row = lax.axis_index("row")
    col = lax.axis_index("col")
    zlo, y, x = row // 16, (row // 4) % 4, row % 4
    zhi, core = col // 2, col % 2
    z = zhi * 4 + zlo
    sibling = (row, zhi * 2 + (1 - core))

    def at_z(zz, kk):
        zz = zz % 16
        return ((zz % 4) * 16 + y * 4 + x, (zz // 4) * 2 + kk)

    def at_xy(xx, yy, kk):
        return (zlo * 16 + (yy % 4) * 4 + xx % 4, zhi * 2 + kk)

    def in_plane(m):
        return (x + m % 4) % 4, (y + m // 4) % 4

    barrier = pltpu.get_barrier_semaphore()

    def greet(dev):
        pl.semaphore_signal(barrier, inc=1, device_id=dev, device_id_type=MESH)

    for m in range(1, 16):
        xx, yy = in_plane(m)
        greet(at_xy(xx, yy, core))
        greet(at_xy(xx, yy, 1 - core))
        greet(at_z(z + m, core))
    greet(sibling)

    def cols(h, k=None):
        start = ((h % 4) * 2 + (core if k is None else k)) * 16
        return pl.ds(pl.multiple_of(start, 16), 16)

    half = pl.ds(0, 64)
    loads = [pltpu.make_async_copy(
        blocks.at[:, pl.ds(pl.multiple_of(64 * x, 64), 64)], raw.at[:, half], loc_sem.at[0])]
    for s in range(4):
        loads.append(pltpu.make_async_copy(
            blocks.at[:, pl.ds(pl.multiple_of(64 * s + 16 * y, 16), 16)],
            raw.at[:, pl.ds(64 + 16 * s, 16)], loc_sem.at[1 + s]))
    for load in loads:
        load.start()
    rows = lax.broadcasted_iota(jnp.int32, (128, 128), 0)
    lanes = lax.broadcasted_iota(jnp.int32, (128, 128), 1)
    source = lax.broadcasted_iota(jnp.int32, (512, 128), 0)
    target = lax.broadcasted_iota(jnp.int32, (512, 128), 1)
    place = target // 64 * 256 + target // 16 % 4 * 64 + target % 16
    for yy in range(4):
        order = jnp.where(source == place + 16 * yy, 1.0, 0.0).astype(jnp.bfloat16)
        w4[yy] = jnp.dot(wt[...], order, preferred_element_type=jnp.float32).astype(jnp.bfloat16)
    entry = jnp.broadcast_to(pos[...].astype(jnp.float32), (128, 128))
    own_q[...] = jnp.where(entry.T == (2 * col + lanes // 64).astype(jnp.float32), 1.0, 0.0)
    for load in loads:
        load.wait()

    @pl.loop(0, 16)
    def _(j):
        start = pl.multiple_of(j * PITCH, 8)
        for side in range(2):
            wide[side, pl.ds(start, 128)] = raw[j, :, 128 * side : 128 * side + 128].astype(jnp.float32)

    def one_row(r):
        return jnp.concatenate(
            [wide[side, pl.ds(r, 16, stride=PITCH)] for side in range(2)], axis=1
        ).astype(jnp.bfloat16)

    @pl.loop(0, 64, step=8)
    def _(r):
        for s in range(8):
            ga[r + s, cols(zhi)] = one_row(r + s)
            gd[r + s, cols(zhi)] = one_row(64 + r + s)

    pl.semaphore_wait(barrier, 46)

    quarter = 4 * zlo

    def share_rows(t, h):
        return (
            ga.at[pl.ds(16 * y + t, 4), cols(h)],
            gd.at[pl.ds(16 * x + t, 4), cols(h)],
        )

    own_part = share_rows(quarter, zhi)[0]
    for item in ITEMS:
        remote(own_part, own_part, z_send.at[item], z_recv.at[item], at_z(z + 4 * item, core)).start()

    for m in range(1, 4):
        remote(xt, xp.at[y], x_send, x_recv, at_xy(x, y + m, core)).start()
    for m in range(1, 16):
        xx, yy = in_plane(m)
        remote(w4.at[yy], wp.at[y * 4 + x], w_send, w_recv, at_xy(xx, yy, core)).start()
    pltpu.make_async_copy(xt, xp.at[y], loc_sem.at[0]).start()
    pltpu.make_async_copy(w4.at[y], wp.at[y * 4 + x], loc_sem.at[1]).start()

    own_a, own_d = ga.at[:, cols(zhi)], gd.at[:, cols(zhi)]
    remote(own_a, own_a, sa_send.at[0], sa_recv.at[0], sibling).start()
    remote(own_d, own_d, sd_send.at[0], sd_recv.at[0], sibling).start()

    def multiply(h, k):
        keep = jnp.concatenate([own_q[cols(h, k)]] * 4, axis=1) > 0.5

        @pl.loop(0, 64, step=32)
        def _(d):
            g = gd[pl.ds(d, 32), cols(h, k)].reshape(512, BLOCK)
            full = lax.dot_general(
                g, xw[...], (((1,), (1,)), ((), ())), preferred_element_type=jnp.float32
            ).reshape(32, 16, 512)
            rbuf[pl.ds(d, 32), cols(h, k)] = jnp.where(keep[None], full, 0.0).astype(jnp.bfloat16)

    def spread(t, item):
        a_part, d_part = share_rows(t, zhi + 4 - item)
        for m in range(1, 4):
            remote(a_part, a_part, ya_send.at[item], ya_recv.at[item], at_xy(x, y + m, core)).start()
            remote(a_part, d_part, xd_send.at[item], xd_recv.at[item], at_xy(x + m, y, core)).start()
        pltpu.make_async_copy(a_part, d_part, cp_sem.at[item]).start()

    def hand_over(item):
        await_bytes(ga.at[pl.ds(0, 48), pl.ds(0, 16)], ya_recv.at[item])
        part_a = ga.at[:, cols(zhi + 4 - item)]
        remote(part_a, part_a, sa_send.at[item], sa_recv.at[item], sibling).start()
        await_bytes(ga.at[pl.ds(0, 48), pl.ds(0, 16)], xd_recv.at[item])
        await_bytes(ga.at[pl.ds(0, 16), pl.ds(0, 16)], cp_sem.at[item])
        part_d = gd.at[:, cols(zhi + 4 - item)]
        remote(part_d, part_d, sd_send.at[item], sd_recv.at[item], sibling).start()

    for item in ITEMS:
        a_part, _ = share_rows(quarter, zhi + 4 - item)
        if item == ITEMS[0]:
            pltpu.make_async_copy(xt, xp.at[y], loc_sem.at[0]).wait()
            pltpu.make_async_copy(w4.at[y], wp.at[y * 4 + x], loc_sem.at[1]).wait()
            await_bytes(xp.at[pl.ds(0, 3)], x_recv)
            for p in range(4):
                for q in range(2):
                    xw[128 * p + 64 * q : 128 * p + 64 * q + 64] = xp[p, :, BLOCK * q : BLOCK * q + BLOCK]
            multiply(zhi, core)
        await_bytes(a_part, z_recv.at[item])
        for m in range(1, 4):
            plane = zhi * 4 + (zlo + m) % 4
            remote(a_part, a_part, v_send.at[item], v_recv.at[item, m], at_z(plane, core)).start()
        spread(quarter, item)
    await_bytes(own_a, sa_recv.at[0])
    await_bytes(own_d, sd_recv.at[0])
    multiply(zhi, 1 - core)
    await_bytes(wp.at[pl.ds(0, 15)], w_recv)
    for p in range(4):
        ww[128 * p : 128 * p + 128] = (
            wp[4 * p : 4 * p + 4].reshape(BLOCK, 128).astype(jnp.float32).T.astype(jnp.bfloat16)
        )
    for item in ITEMS:
        for m in range(1, 4):
            t = 4 * ((zlo + 4 - m) % 4)
            await_bytes(share_rows(t, zhi)[0], v_recv.at[item, m])
            spread(t, item)
    for item in ITEMS:
        hand_over(item)
        multiply(zhi + 4 - item, core)
    for item in ITEMS:
        await_bytes(own_a, sa_recv.at[item])
        await_bytes(own_d, sd_recv.at[item])
        multiply(zhi + 4 - item, 1 - core)

    at_p = [pos[...] == 4 * zlo + p for p in range(4)]

    def pick(values, lane):
        total = None
        for p in range(4):
            term = jnp.where(at_p[p], values[128 * p : 128 * p + 128, lane : lane + 128], 0.0)
            total = term if total is None else total + term
        return total

    @pl.loop(0, 64, step=2)
    def _(a):
        g = ga[pl.ds(a, 2)].reshape(256, BLOCK)
        full = lax.dot_general(
            ww[...], g, (((1,), (1,)), ((), ())), preferred_element_type=jnp.float32
        )
        for s in range(2):
            lbuf[pl.ds(pl.multiple_of((a + s) * PITCH, 8), 128)] = pick(full, 128 * s)

    acc[...] = jnp.zeros_like(acc)

    @pl.loop(0, 64, step=4)
    def _(d):
        right = jnp.concatenate(
            [lbuf[pl.ds(q * 64 + d + s, 64, stride=PITCH)].astype(jnp.bfloat16)
             for s in range(4) for q in range(2)], axis=0)
        tiles = [rbuf[d + s] for s in range(4)]
        left = jnp.concatenate(
            [jnp.concatenate([t[:, 128 * p : 128 * p + 128] for t in tiles], axis=1) for p in range(4)],
            axis=0)
        acc[...] += jnp.dot(left, right, preferred_element_type=jnp.float32)

    part[...] = pick(acc[...], 0).T

    me = y * 4 + x
    mine = pl.ds(pl.multiple_of(8 * me, 8), 8)
    for m in range(16):
        xx, yy = in_plane(m)
        theirs = part.at[pl.ds(8 * (yy * 4 + xx), 8)]
        if m:
            remote(theirs, rs.at[core * 16 + me], red_send.at[0], red_recv.at[0], at_xy(xx, yy, core)).start()
        remote(theirs, rs.at[core * 16 + me], red_send.at[0], red_recv.at[0], at_xy(xx, yy, 1 - core)).start()
    rs[core * 16 + me] = part[mine]
    await_bytes(rs.at[pl.ds(0, 31)], red_recv.at[0])
    share[...] = jnp.sum(rs[...], axis=0)
    for m in range(1, 16):
        remote(share, zs.at[z], red_send.at[1], red_recv.at[1], at_z(z + m, core)).start()
    zs[z] = share[...]
    await_bytes(zs.at[pl.ds(0, 15)], red_recv.at[1])
    await_bytes(rs.at[pl.ds(0, 31)], red_send.at[0])
    await_bytes(zs.at[pl.ds(0, 15)], red_send.at[1])
    share[...] = jnp.sum(zs[...], axis=0)
    whole = acc.at[pl.ds(0, 128)]
    for m in range(1, 16):
        xx, yy = in_plane(m)
        remote(share, whole.at[mine], red_send.at[2], red_recv.at[2], at_xy(xx, yy, core)).start()
    whole[mine] = share[...]
    await_bytes(zs.at[pl.ds(0, 15)], red_recv.at[2])
    await_bytes(zs.at[pl.ds(0, 15)], red_send.at[2])

    schur = whole[...]
    factor = jnp.zeros((128, 128), jnp.float32)
    width = 8
    for k in range(PANELS * width):
        lo = k // width * width
        if k == lo:
            inside = (rows >= lo) & (rows < lo + width) & (lanes >= lo) & (lanes < lo + width)
            schur = jnp.where(inside, 0.5 * (schur + schur.T), schur)
        column = jnp.sum(jnp.where(lanes == k, schur, 0.0), axis=1, keepdims=True)
        pivot = jnp.sum(jnp.where(rows[:, :1] == k, column, 0.0), axis=0, keepdims=True)
        column = jnp.where(rows[:, :1] >= k, column / jnp.sqrt(pivot), 0.0)
        line = jnp.sum(jnp.where(rows == lanes, column, 0.0), axis=0, keepdims=True)
        schur = schur - column * line
        factor = jnp.where(lanes == k, column, factor)
    bound = PANELS * width
    part[...] = factor
    near = pl.ds(pl.multiple_of(row // 4 * 8, 8), 8)
    up = (8 - 2 * (row % 4)) % 8
    factor_ref[...] = pltpu.roll(part[near], up, 0)[:2, :bound]
    part[...] = jnp.where((rows >= bound) & (lanes >= bound), schur, 0.0)
    shifted = pltpu.roll(pltpu.roll(part[near], up, 0), (128 - 16 * col) % 128, 1)
    reduced_ref[...] = shifted[:2, :16]

    await_bytes(xp.at[pl.ds(0, 3)], x_send)
    await_bytes(wp.at[pl.ds(0, 15)], w_send)
    for item in ITEMS:
        await_bytes(ga.at[pl.ds(0, 4), pl.ds(0, 16)], z_send.at[item])
        await_bytes(ga.at[pl.ds(0, 12), pl.ds(0, 16)], v_send.at[item])
        await_bytes(ga.at[pl.ds(0, 48), pl.ds(0, 16)], ya_send.at[item])
        await_bytes(ga.at[pl.ds(0, 48), pl.ds(0, 16)], xd_send.at[item])
    for item in range(4):
        await_bytes(ga.at[:, pl.ds(0, 16)], sa_send.at[item])
        await_bytes(gd.at[:, pl.ds(0, 16)], sd_send.at[item])


def on_device(blocks, position, primal, dual_inverse):
    tile_cols = blocks.shape[0]
    rows, width = primal.shape
    per_row = tile_cols * lax.axis_size("col") // lax.axis_size("row")
    count = position.shape[0]
    vmem = pl.BlockSpec(memory_space=pltpu.VMEM)
    hbm = pl.BlockSpec(memory_space=pl.ANY)
    bf, f32 = jnp.bfloat16, jnp.float32
    dma = pltpu.SemaphoreType.DMA
    return pl.pallas_call(
        schur_kernel,
        out_shape=(
            jax.ShapeDtypeStruct((per_row, PANELS * 8), f32),
            jax.ShapeDtypeStruct((per_row, tile_cols), f32),
        ),
        in_specs=[hbm, vmem, vmem, vmem],
        out_specs=(vmem, vmem),
        scratch_shapes=[
            pltpu.VMEM((tile_cols, 128, BLOCK), bf),
            pltpu.VMEM((2, tile_cols * PITCH, 128), f32),
            pltpu.VMEM((4, rows, 128), bf),
            pltpu.VMEM((64, count, BLOCK), bf),
            pltpu.VMEM((64, count, BLOCK), bf),
            pltpu.VMEM((4, rows, width), bf),
            pltpu.VMEM((16, rows, 128), bf),
            pltpu.VMEM((512, BLOCK), bf),
            pltpu.VMEM((512, BLOCK), bf),
            pltpu.VMEM((count, 128), f32),
            pltpu.VMEM((64, count, 512), bf),
            pltpu.VMEM((64 * PITCH, 128), f32),
            pltpu.VMEM((512, count), f32),
            pltpu.VMEM((count, count), f32),
            pltpu.VMEM((8, count), f32),
            pltpu.VMEM((32, 8, count), f32),
            pltpu.VMEM((16, 8, count), f32),
            dma((5,)), dma, dma, dma, dma,
            dma((4,)), dma((4,)), dma((4,)), dma((4, 4)),
            dma((4,)), dma((4,)), dma((4,)), dma((4,)), dma((4,)),
            dma((4,)), dma((4,)), dma((4,)), dma((4,)), dma((3,)), dma((3,)),
        ],
        compiler_params=pltpu.CompilerParams(
            collective_id=0, has_side_effects=True, vmem_limit_bytes=56 << 20
        ),
        name="schur",
    )(blocks, primal, dual_inverse, position.reshape(1, count))


def solution(mesh):
    in_specs = (P("col", None, None), P(), P("row", "col"), P("row", "col"))
    out_specs = (P("row", None), P("row", "col"))
    return jax.shard_map(
        on_device, mesh=mesh, in_specs=in_specs, out_specs=out_specs, check_vma=False
    )
```

```python
import functools

import jax
import jax.numpy as jnp
from jax import lax
from jax.experimental import pallas as pl
from jax.experimental.pallas import tpu as pltpu
from jax.sharding import PartitionSpec as P

BLOCK = 256
PANELS = 2
MESH = pl.DeviceIdType.MESH
ITEMS = (1, 3, 2)
PITCH = 136


def remote(src, dst, send, recv, dev):
    return pltpu.make_async_remote_copy(
        src_ref=src, dst_ref=dst, send_sem=send, recv_sem=recv, device_id=dev, device_id_type=MESH
    )


def await_bytes(ref, sem):
    pltpu.make_async_copy(ref, ref, sem).wait()


def schur_kernel(
    blocks, xt, wt, pos,
    factor_ref, reduced_ref,
    raw, wide, w4, ga, gd, xp, wp, xw, ww, own_q, rbuf, lbuf, acc, part, share, rs, zs,
    loc_sem, x_send, x_recv, w_send, w_recv, near_send, near_recv, pass_send, z_send, z_recv, v_send, v_recv,
    ya_send, xd_send, ya_recv, xd_recv, yy_recv, xx_recv, cp_sem, sa_send, sd_send, sa_recv, sd_recv, red_send, red_recv,
):
    row = lax.axis_index("row")
    col = lax.axis_index("col")
    zlo, y, x = row // 16, (row // 4) % 4, row % 4
    zhi, core = col // 2, col % 2
    z = zhi * 4 + zlo
    sibling = (row, zhi * 2 + (1 - core))

    def at_z(zz, kk):
        zz = zz % 16
        return ((zz % 4) * 16 + y * 4 + x, (zz // 4) * 2 + kk)

    def at_xy(xx, yy, kk):
        return (zlo * 16 + (yy % 4) * 4 + xx % 4, zhi * 2 + kk)

    def in_plane(m):
        return (x + m % 4) % 4, (y + m // 4) % 4

    barrier = pltpu.get_barrier_semaphore()

    def greet(dev):
        pl.semaphore_signal(barrier, inc=1, device_id=dev, device_id_type=MESH)

    for m in range(1, 16):
        xx, yy = in_plane(m)
        greet(at_xy(xx, yy, core))
        greet(at_xy(xx, yy, 1 - core))
        greet(at_z(z + m, core))
    greet(sibling)

    def cols(h, k=None):
        start = ((h % 4) * 2 + (core if k is None else k)) * 16
        return pl.ds(pl.multiple_of(start, 16), 16)

    half = pl.ds(0, 64)
    loads = [pltpu.make_async_copy(
        blocks.at[:, pl.ds(pl.multiple_of(64 * x, 64), 64)], raw.at[:, half], loc_sem.at[0])]
    for s in range(4):
        loads.append(pltpu.make_async_copy(
            blocks.at[:, pl.ds(pl.multiple_of(64 * s + 16 * y, 16), 16)],
            raw.at[:, pl.ds(64 + 16 * s, 16)], loc_sem.at[1 + s]))
    for load in loads:
        load.start()
    rows = lax.broadcasted_iota(jnp.int32, (128, 128), 0)
    lanes = lax.broadcasted_iota(jnp.int32, (128, 128), 1)
    source = lax.broadcasted_iota(jnp.int32, (512, 128), 0)
    target = lax.broadcasted_iota(jnp.int32, (512, 128), 1)
    place = target // 64 * 256 + target // 16 % 4 * 64 + target % 16
    for yy in range(4):
        order = jnp.where(source == place + 16 * yy, 1.0, 0.0).astype(jnp.bfloat16)
        w4[yy] = jnp.dot(wt[...], order, preferred_element_type=jnp.float32).astype(jnp.bfloat16)
    entry = jnp.broadcast_to(pos[...].astype(jnp.float32), (128, 128))
    own_q[...] = jnp.where(entry.T == (2 * col + lanes // 64).astype(jnp.float32), 1.0, 0.0)
    for load in loads:
        load.wait()

    @pl.loop(0, 16)
    def _(j):
        start = pl.multiple_of(j * PITCH, 8)
        for side in range(2):
            wide[side, pl.ds(start, 128)] = raw[j, :, 128 * side : 128 * side + 128].astype(jnp.float32)

    def one_row(r):
        return jnp.concatenate(
            [wide[side, pl.ds(r, 16, stride=PITCH)] for side in range(2)], axis=1
        ).astype(jnp.bfloat16)

    @pl.loop(0, 64, step=8)
    def _(r):
        for s in range(8):
            ga[r + s, cols(zhi)] = one_row(r + s)
            gd[r + s, cols(zhi)] = one_row(64 + r + s)

    pl.semaphore_wait(barrier, 46)

    quarter = 4 * zlo

    def share_rows(t, h):
        return (
            ga.at[pl.ds(16 * y + t, 4), cols(h)],
            gd.at[pl.ds(16 * x + t, 4), cols(h)],
        )

    own_part = share_rows(quarter, zhi)[0]

    remote(own_part, own_part, z_send, z_recv, at_z(z + 8, core)).start()

    def near(way, item, planes):
        for t in range(0, 16, 4):
            piece = share_rows(t, zhi)[0]
            for v in planes:
                remote(piece, piece, near_send.at[way], near_recv.at[item, t // 4],
                       at_z(4 * (zhi + item) + v, core)).start()

    @pl.when(zlo == 3)
    def _():
        near(0, 1, (0, 2))

    @pl.when(zlo == 0)
    def _():
        near(1, 3, (3, 1))


    for way, step in ((0, 1), (1, 3)):
        remote(xt, xp.at[y], x_send, x_recv.at[way], at_xy(x, y + step, core)).start()
    for m in range(1, 4):
        yy = (y + m) % 4
        remote(w4.at[yy], wp.at[x, y], w_send.at[0], w_recv.at[0], at_xy(x, yy, core)).start()
    pltpu.make_async_copy(xt, xp.at[y], loc_sem.at[0]).start()
    pltpu.make_async_copy(w4.at[y], wp.at[x, y], loc_sem.at[1]).start()

    own_a, own_d = ga.at[:, cols(zhi)], gd.at[:, cols(zhi)]
    remote(own_a, own_a, sa_send.at[0], sa_recv.at[0], sibling).start()
    remote(own_d, own_d, sd_send.at[0], sd_recv.at[0], sibling).start()

    def multiply(h, k):
        keep = jnp.concatenate([own_q[cols(h, k)]] * 4, axis=1) > 0.5

        @pl.loop(0, 64, step=32)
        def _(d):
            g = gd[pl.ds(d, 32), cols(h, k)].reshape(512, BLOCK)
            full = lax.dot_general(
                g, xw[...], (((1,), (1,)), ((), ())), preferred_element_type=jnp.float32
            ).reshape(32, 16, 512)
            rbuf[pl.ds(d, 32), cols(h, k)] = jnp.where(keep[None], full, 0.0).astype(jnp.bfloat16)

    def spread(t, item):
        a_part, d_part = share_rows(t, zhi + 4 - item)
        part_half = t // 8
        for way, step in ((0, 1), (1, 3)):
            remote(a_part, a_part, ya_send.at[item], ya_recv.at[item, way, part_half],
                   at_xy(x, y + step, core)).start()
            remote(a_part, d_part, xd_send.at[item], xd_recv.at[item, way, part_half],
                   at_xy(x + step, y, core)).start()
        pltpu.make_async_copy(a_part, d_part, cp_sem.at[item]).start()

    eight = ga.at[pl.ds(0, 8), pl.ds(0, 16)]

    def pass_on(item):
        for way, step in ((0, 1), (1, 3)):
            back = 4 - step
            a_part = ga.at[pl.ds((y + back) % 4 * 16 + 8 * way, 8), cols(zhi + 4 - item)]
            await_bytes(eight, ya_recv.at[item, way, way])
            remote(a_part, a_part, ya_send.at[item], yy_recv.at[item], at_xy(x, y + step, core)).start()
            d_part = gd.at[pl.ds((x + back) % 4 * 16 + 8 * way, 8), cols(zhi + 4 - item)]
            await_bytes(eight, xd_recv.at[item, way, way])
            remote(d_part, d_part, xd_send.at[item], xx_recv.at[item], at_xy(x + step, y, core)).start()

    def hand_over(item):
        for way in range(2):
            await_bytes(eight, ya_recv.at[item, way, 1 - way])
        await_bytes(ga.at[pl.ds(0, 16), pl.ds(0, 16)], yy_recv.at[item])
        part_a = ga.at[:, cols(zhi + 4 - item)]
        remote(part_a, part_a, sa_send.at[item], sa_recv.at[item], sibling).start()
        for way in range(2):
            await_bytes(eight, xd_recv.at[item, way, 1 - way])
        await_bytes(ga.at[pl.ds(0, 16), pl.ds(0, 16)], xx_recv.at[item])
        await_bytes(ga.at[pl.ds(0, 16), pl.ds(0, 16)], cp_sem.at[item])
        part_d = gd.at[:, cols(zhi + 4 - item)]
        remote(part_d, part_d, sd_send.at[item], sd_recv.at[item], sibling).start()

    odd = zlo % 2
    early, late = 1 + 2 * odd, 3 - 2 * odd
    onward = at_z(z + 17 - 2 * odd, core)

    def from_early(t):
        await_bytes(own_part, near_recv.at[early, t // 4])
        piece = share_rows(t, zhi + 4 - early)[0]
        remote(piece, piece, pass_send, near_recv.at[early, t // 4], onward).start()
        spread(t, early)

    def from_late(t):
        await_bytes(own_part, near_recv.at[late, t // 4])
        spread(t, late)

    def from_far():
        a_part, _ = share_rows(quarter, zhi + 2)
        await_bytes(a_part, z_recv)
        for m in range(1, 4):
            plane = zhi * 4 + (zlo + m) % 4
            remote(a_part, a_part, v_send, v_recv.at[m], at_z(plane, core)).start()
        spread(quarter, 2)

    def from_planes():
        for m in range(1, 4):
            t = 4 * ((zlo + 4 - m) % 4)
            await_bytes(own_part, v_recv.at[m])
            spread(t, 2)

    for way, step in ((0, 1), (1, 3)):
        x_part = xp.at[(y + 4 - step) % 4, pl.ds(32 * way, 32)]
        await_bytes(xp.at[0], x_recv.at[way])
        remote(x_part, x_part, x_send, x_recv.at[2], at_xy(x, y + step, core)).start()
    pltpu.make_async_copy(w4.at[y], wp.at[x, y], loc_sem.at[1]).wait()
    await_bytes(wp.at[0, pl.ds(0, 3)], w_recv.at[0])
    for m in range(1, 4):
        remote(wp.at[x], wp.at[x], w_send.at[1], w_recv.at[1], at_xy(x + m, y, core)).start()
    from_early(0)
    pltpu.make_async_copy(xt, xp.at[y], loc_sem.at[0]).wait()
    await_bytes(xp.at[0], x_recv.at[2])
    for p in range(4):
        for q in range(2):
            xw[128 * p + 64 * q : 128 * p + 64 * q + 64] = xp[p, :, BLOCK * q : BLOCK * q + BLOCK]
    multiply(zhi, core)
    from_early(4)
    from_late(0)
    from_far()
    from_early(8)
    from_late(4)
    from_early(12)
    from_late(8)
    from_late(12)
    from_planes()
    pass_on(early)
    pass_on(late)
    pass_on(2)
    await_bytes(own_a, sa_recv.at[0])
    await_bytes(own_d, sd_recv.at[0])
    multiply(zhi, 1 - core)
    await_bytes(wp.at[pl.ds(0, 3)], w_recv.at[1])
    for p in range(4):
        ww[128 * p : 128 * p + 128] = (
            wp[:, p].reshape(BLOCK, 128).astype(jnp.float32).T.astype(jnp.bfloat16)
        )
    for item in (early, late, 2):
        hand_over(item)
        multiply(zhi + 4 - item, core)
    for item in (early, late, 2):
        await_bytes(own_a, sa_recv.at[item])
        await_bytes(own_d, sd_recv.at[item])
        multiply(zhi + 4 - item, 1 - core)

    at_p = [pos[...] == 4 * zlo + p for p in range(4)]

    def pick(values, lane):
        total = None
        for p in range(4):
            term = jnp.where(at_p[p], values[128 * p : 128 * p + 128, lane : lane + 128], 0.0)
            total = term if total is None else total + term
        return total

    @pl.loop(0, 64, step=4)
    def _(a):
        g = ga[pl.ds(a, 4)].reshape(512, BLOCK)
        full = lax.dot_general(
            ww[...], g, (((1,), (1,)), ((), ())), preferred_element_type=jnp.float32
        )
        for s in range(4):
            lbuf[pl.ds(pl.multiple_of((a + s) * PITCH, 8), 128)] = pick(full, 128 * s)

    acc[...] = jnp.zeros_like(acc)

    @pl.loop(0, 64, step=4)
    def _(d):
        right = jnp.concatenate(
            [lbuf[pl.ds(q * 64 + d + s, 64, stride=PITCH)].astype(jnp.bfloat16)
             for s in range(4) for q in range(2)], axis=0)
        tiles = [rbuf[d + s] for s in range(4)]
        left = jnp.concatenate(
            [jnp.concatenate([t[:, 128 * p : 128 * p + 128] for t in tiles], axis=1) for p in range(4)],
            axis=0)
        acc[...] += jnp.dot(left, right, preferred_element_type=jnp.float32)

    part[...] = pick(acc[...], 0).T

    me = y * 4 + x
    mine = pl.ds(pl.multiple_of(8 * me, 8), 8)
    for m in range(16):
        xx, yy = in_plane(m)
        theirs = part.at[pl.ds(8 * (yy * 4 + xx), 8)]
        if m:
            remote(theirs, rs.at[core * 16 + me], red_send.at[0], red_recv.at[0], at_xy(xx, yy, core)).start()
        remote(theirs, rs.at[core * 16 + me], red_send.at[0], red_recv.at[0], at_xy(xx, yy, 1 - core)).start()
    rs[core * 16 + me] = part[mine]
    await_bytes(rs.at[pl.ds(0, 31)], red_recv.at[0])
    share[...] = jnp.sum(rs[...], axis=0)
    for m in range(1, 16):
        remote(share, zs.at[z], red_send.at[1], red_recv.at[1], at_z(z + m, core)).start()
    zs[z] = share[...]
    await_bytes(zs.at[pl.ds(0, 15)], red_recv.at[1])
    await_bytes(rs.at[pl.ds(0, 31)], red_send.at[0])
    await_bytes(zs.at[pl.ds(0, 15)], red_send.at[1])
    share[...] = jnp.sum(zs[...], axis=0)
    whole = acc.at[pl.ds(0, 128)]
    for m in range(1, 16):
        xx, yy = in_plane(m)
        remote(share, whole.at[mine], red_send.at[2], red_recv.at[2], at_xy(xx, yy, core)).start()
    whole[mine] = share[...]
    await_bytes(zs.at[pl.ds(0, 15)], red_recv.at[2])
    await_bytes(zs.at[pl.ds(0, 15)], red_send.at[2])

    schur = whole[...]
    factor = jnp.zeros((128, 128), jnp.float32)
    width = 8
    for k in range(PANELS * width):
        lo = k // width * width
        if k == lo:
            inside = (rows >= lo) & (rows < lo + width) & (lanes >= lo) & (lanes < lo + width)
            schur = jnp.where(inside, 0.5 * (schur + schur.T), schur)
        column = jnp.sum(jnp.where(lanes == k, schur, 0.0), axis=1, keepdims=True)
        pivot = jnp.sum(jnp.where(rows[:, :1] == k, column, 0.0), axis=0, keepdims=True)
        column = jnp.where(rows[:, :1] >= k, column / jnp.sqrt(pivot), 0.0)
        line = jnp.sum(jnp.where(rows == lanes, column, 0.0), axis=0, keepdims=True)
        schur = schur - column * line
        factor = jnp.where(lanes == k, column, factor)
    bound = PANELS * width
    part[...] = factor
    near = pl.ds(pl.multiple_of(row // 4 * 8, 8), 8)
    up = (8 - 2 * (row % 4)) % 8
    factor_ref[...] = pltpu.roll(part[near], up, 0)[:2, :bound]
    part[...] = jnp.where((rows >= bound) & (lanes >= bound), schur, 0.0)
    shifted = pltpu.roll(pltpu.roll(part[near], up, 0), (128 - 16 * col) % 128, 1)
    reduced_ref[...] = shifted[:2, :16]

    await_bytes(xp.at[pl.ds(0, 3)], x_send)
    await_bytes(wp.at[0, pl.ds(0, 3)], w_send.at[0])
    await_bytes(wp.at[pl.ds(0, 3)], w_send.at[1])
    for item in ITEMS:
        await_bytes(ga.at[pl.ds(0, 48), pl.ds(0, 16)], ya_send.at[item])
        await_bytes(ga.at[pl.ds(0, 48), pl.ds(0, 16)], xd_send.at[item])
    await_bytes(own_part, z_send)
    await_bytes(ga.at[pl.ds(0, 16), pl.ds(0, 16)], pass_send)
    await_bytes(ga.at[pl.ds(0, 12), pl.ds(0, 16)], v_send)

    @pl.when(zlo == 3)
    def _():
        await_bytes(ga.at[pl.ds(0, 32), pl.ds(0, 16)], near_send.at[0])

    @pl.when(zlo == 0)
    def _():
        await_bytes(ga.at[pl.ds(0, 32), pl.ds(0, 16)], near_send.at[1])

    for item in range(4):
        await_bytes(ga.at[:, pl.ds(0, 16)], sa_send.at[item])
        await_bytes(gd.at[:, pl.ds(0, 16)], sd_send.at[item])


def on_device(blocks, position, primal, dual_inverse):
    tile_cols = blocks.shape[0]
    rows, width = primal.shape
    per_row = tile_cols * lax.axis_size("col") // lax.axis_size("row")
    count = position.shape[0]
    vmem = pl.BlockSpec(memory_space=pltpu.VMEM)
    hbm = pl.BlockSpec(memory_space=pl.ANY)
    bf, f32 = jnp.bfloat16, jnp.float32
    dma = pltpu.SemaphoreType.DMA
    return pl.pallas_call(
        schur_kernel,
        out_shape=(
            jax.ShapeDtypeStruct((per_row, PANELS * 8), f32),
            jax.ShapeDtypeStruct((per_row, tile_cols), f32),
        ),
        in_specs=[hbm, vmem, vmem, vmem],
        out_specs=(vmem, vmem),
        scratch_shapes=[
            pltpu.VMEM((tile_cols, 128, BLOCK), bf),
            pltpu.VMEM((2, tile_cols * PITCH, 128), f32),
            pltpu.VMEM((4, rows, 128), bf),
            pltpu.VMEM((64, count, BLOCK), bf),
            pltpu.VMEM((64, count, BLOCK), bf),
            pltpu.VMEM((4, rows, width), bf),
            pltpu.VMEM((4, 4, rows, 128), bf),
            pltpu.VMEM((512, BLOCK), bf),
            pltpu.VMEM((512, BLOCK), bf),
            pltpu.VMEM((count, 128), f32),
            pltpu.VMEM((64, count, 512), bf),
            pltpu.VMEM((64 * PITCH, 128), f32),
            pltpu.VMEM((512, count), f32),
            pltpu.VMEM((count, count), f32),
            pltpu.VMEM((8, count), f32),
            pltpu.VMEM((32, 8, count), f32),
            pltpu.VMEM((16, 8, count), f32),
            dma((5,)), dma, dma((3,)), dma((2,)), dma((2,)),
            dma((2,)), dma((4, 4)), dma, dma, dma, dma, dma((4,)),
            dma((4,)), dma((4,)), dma((4, 2, 2)), dma((4, 2, 2)), dma((4,)), dma((4,)), dma((4,)),
            dma((4,)), dma((4,)), dma((4,)), dma((4,)), dma((3,)), dma((3,)),
        ],
        compiler_params=pltpu.CompilerParams(
            collective_id=0, has_side_effects=True, vmem_limit_bytes=56 << 20
        ),
        name="schur",
    )(blocks, primal, dual_inverse, position.reshape(1, count))


def solution(mesh):
    in_specs = (P("col", None, None), P(), P("row", "col"), P("row", "col"))
    out_specs = (P("row", None), P("row", "col"))
    return jax.shard_map(
        on_device, mesh=mesh, in_specs=in_specs, out_specs=out_specs, check_vma=False
    )
```

```python
import functools

import jax
import jax.numpy as jnp
from jax import lax
from jax.experimental import pallas as pl
from jax.experimental.pallas import tpu as pltpu
from jax.sharding import PartitionSpec as P

BLOCK = 256
PANELS = 2
MESH = pl.DeviceIdType.MESH
ITEMS = (1, 3, 2)
PITCH = 136


def remote(src, dst, send, recv, dev):
    return pltpu.make_async_remote_copy(
        src_ref=src, dst_ref=dst, send_sem=send, recv_sem=recv, device_id=dev, device_id_type=MESH
    )


def await_bytes(ref, sem):
    pltpu.make_async_copy(ref, ref, sem).wait()


def schur_kernel(
    blocks, xt, wt, pos,
    out_ref,
    raw, wide, w4, ga, gd, xp, wp, xw, ww, own_q, rbuf, lbuf, acc, part, other, both, share, rs, zs,
    loc_sem, x_send, x_recv, w_send, w_recv, near_send, near_recv, pass_send, z_send, z_recv, v_send, v_recv,
    ya_send, xd_send, ya_recv, xd_recv, yy_recv, xx_recv, cp_sem, sa_send, sd_send, sa_recv, sd_recv, red_send, red_recv,
):
    row = lax.axis_index("row")
    col = lax.axis_index("col")
    zlo, y, x = row // 16, (row // 4) % 4, row % 4
    zhi, core = col // 2, col % 2
    z = zhi * 4 + zlo
    sibling = (row, zhi * 2 + (1 - core))

    def at_z(zz, kk):
        zz = zz % 16
        return ((zz % 4) * 16 + y * 4 + x, (zz // 4) * 2 + kk)

    def at_xy(xx, yy, kk):
        return (zlo * 16 + (yy % 4) * 4 + xx % 4, zhi * 2 + kk)

    def in_plane(m):
        return (x + m % 4) % 4, (y + m // 4) % 4

    barrier = pltpu.get_barrier_semaphore()

    def greet(dev):
        pl.semaphore_signal(barrier, inc=1, device_id=dev, device_id_type=MESH)

    for m in range(1, 16):
        xx, yy = in_plane(m)
        greet(at_xy(xx, yy, core))
        greet(at_z(z + m, core))
    greet(sibling)

    def cols(h, k=None):
        start = ((h % 4) * 2 + (core if k is None else k)) * 16
        return pl.ds(pl.multiple_of(start, 16), 16)

    first = pltpu.make_async_copy(
        blocks.at[:, pl.ds(pl.multiple_of(64 * x + 16 * y, 16), 16)], raw.at[:, pl.ds(128, 16)], loc_sem.at[5])
    first.start()
    loads = [pltpu.make_async_copy(
        blocks.at[:, pl.ds(pl.multiple_of(64 * x, 64), 64)], raw.at[:, pl.ds(0, 64)], loc_sem.at[0])]
    for s in range(4):
        loads.append(pltpu.make_async_copy(
            blocks.at[:, pl.ds(pl.multiple_of(64 * s + 16 * y, 16), 16)],
            raw.at[:, pl.ds(64 + 16 * s, 16)], loc_sem.at[1 + s]))
    for load in loads:
        load.start()

    def one_row(r):
        return jnp.concatenate(
            [wide[side, pl.ds(r, 16, stride=PITCH)] for side in range(2)], axis=1
        ).astype(jnp.bfloat16)

    first.wait()
    for j in range(16):
        for side in range(2):
            wide[side, j * PITCH : j * PITCH + 16] = (
                raw[j, 128:144, 128 * side : 128 * side + 128].astype(jnp.float32))
    for r in range(16):
        line = one_row(r)
        ga[16 * y + r, cols(zhi)] = line
        gd[16 * x + r, cols(zhi)] = line

    pl.semaphore_wait(barrier, 31)

    quarter = 4 * zlo

    def share_rows(t, h):
        return (
            ga.at[pl.ds(16 * y + t, 4), cols(h)],
            gd.at[pl.ds(16 * x + t, 4), cols(h)],
        )

    own_part = share_rows(quarter, zhi)[0]

    remote(own_part, own_part, z_send, z_recv, at_z(z + 8, core)).start()

    def near(way, item, planes):
        for t in range(0, 16, 4):
            piece = share_rows(t, zhi)[0]
            for v in planes:
                remote(piece, piece, near_send.at[way], near_recv.at[item, t // 4],
                       at_z(4 * (zhi + item) + v, core)).start()

    @pl.when(zlo == 3)
    def _():
        near(0, 1, (0, 2))

    @pl.when(zlo == 0)
    def _():
        near(1, 3, (3, 1))


    for way, step in ((0, 1), (1, 3)):
        remote(xt, xp.at[y], x_send, x_recv.at[way], at_xy(x, y + step, core)).start()
    pltpu.make_async_copy(xt, xp.at[y], loc_sem.at[6]).start()

    rows = lax.broadcasted_iota(jnp.int32, (128, 128), 0)
    lanes = lax.broadcasted_iota(jnp.int32, (128, 128), 1)
    source = lax.broadcasted_iota(jnp.int32, (512, 128), 0)
    target = lax.broadcasted_iota(jnp.int32, (512, 128), 1)
    place = target // 64 * 256 + target // 16 % 4 * 64 + target % 16
    for yy in range(4):
        order = jnp.where(source == place + 16 * yy, 1.0, 0.0).astype(jnp.bfloat16)
        w4[yy] = jnp.dot(wt[...], order, preferred_element_type=jnp.float32).astype(jnp.bfloat16)
    for m in range(1, 4):
        yy = (y + m) % 4
        remote(w4.at[yy], wp.at[x, y], w_send.at[0], w_recv.at[0], at_xy(x, yy, core)).start()
    pltpu.make_async_copy(w4.at[y], wp.at[x, y], loc_sem.at[7]).start()
    for load in loads:
        load.wait()

    @pl.loop(0, 16)
    def _(j):
        start = pl.multiple_of(j * PITCH, 8)
        for side in range(2):
            wide[side, pl.ds(start, 128)] = raw[j, 0:128, 128 * side : 128 * side + 128].astype(jnp.float32)

    for m in range(1, 4):
        a_start, d_start = (y + m) % 4 * 16, (x + m) % 4 * 16

        @pl.loop(0, 16, step=8)
        def _(r):
            for s in range(8):
                ga[a_start + r + s, cols(zhi)] = one_row(a_start + r + s)
                gd[d_start + r + s, cols(zhi)] = one_row(64 + d_start + r + s)

    entry = jnp.broadcast_to(pos[...].astype(jnp.float32), (128, 128))
    own_q[...] = jnp.where(entry.T == (2 * col + lanes // 64).astype(jnp.float32), 1.0, 0.0)

    own_a, own_d = ga.at[:, cols(zhi)], gd.at[:, cols(zhi)]
    remote(own_a, own_a, sa_send.at[0, 0], sa_recv.at[0, 0], sibling).start()
    remote(own_d, own_d, sd_send.at[0], sd_recv.at[0], sibling).start()

    def multiply(h, k):
        keep = jnp.concatenate([own_q[cols(h, k)]] * 4, axis=1) > 0.5

        @pl.loop(0, 64, step=32)
        def _(d):
            g = gd[pl.ds(d, 32), cols(h, k)].reshape(512, BLOCK)
            full = lax.dot_general(
                g, xw[...], (((1,), (1,)), ((), ())), preferred_element_type=jnp.float32
            ).reshape(32, 16, 512)
            rbuf[pl.ds(d, 32), cols(h, k)] = jnp.where(keep[None], full, 0.0).astype(jnp.bfloat16)

    def spread(t, item):
        a_part, d_part = share_rows(t, zhi + 4 - item)
        part_half = t // 8
        for way, step in ((0, 1), (1, 3)):
            remote(a_part, a_part, ya_send.at[item], ya_recv.at[item, way, part_half],
                   at_xy(x, y + step, core)).start()
            remote(a_part, d_part, xd_send.at[item], xd_recv.at[item, way, part_half],
                   at_xy(x + step, y, core)).start()
        pltpu.make_async_copy(a_part, d_part, cp_sem.at[item]).start()

    eight = ga.at[pl.ds(0, 8), pl.ds(0, 16)]

    def pass_on(item):
        for way, step in ((0, 1), (1, 3)):
            back = 4 - step
            a_part = ga.at[pl.ds((y + back) % 4 * 16 + 8 * way, 8), cols(zhi + 4 - item)]
            await_bytes(eight, ya_recv.at[item, way, way])
            remote(a_part, a_part, ya_send.at[item], yy_recv.at[item], at_xy(x, y + step, core)).start()
            d_part = gd.at[pl.ds((x + back) % 4 * 16 + 8 * way, 8), cols(zhi + 4 - item)]
            await_bytes(eight, xd_recv.at[item, way, way])
            remote(d_part, d_part, xd_send.at[item], xx_recv.at[item], at_xy(x + step, y, core)).start()

    sixteen = ga.at[pl.ds(0, 16), pl.ds(0, 16)]

    def hand_rows(item, m):
        part = ga.at[pl.ds((y + m) % 4 * 16, 16), cols(zhi + 4 - item)]
        remote(part, part, sa_send.at[item, m], sa_recv.at[item, m], sibling).start()

    def hand_over(item):
        for way in range(2):
            await_bytes(eight, ya_recv.at[item, way, 1 - way])
            hand_rows(item, 3 - 2 * way)
        await_bytes(sixteen, yy_recv.at[item])
        hand_rows(item, 2)
        for way in range(2):
            await_bytes(eight, xd_recv.at[item, way, 1 - way])
        await_bytes(sixteen, xx_recv.at[item])
        await_bytes(sixteen, cp_sem.at[item])
        part_d = gd.at[:, cols(zhi + 4 - item)]
        remote(part_d, part_d, sd_send.at[item], sd_recv.at[item], sibling).start()

    at_p = [pos[...] == 4 * zlo + p for p in range(4)]

    def pick(values, lane):
        total = None
        for p in range(4):
            term = jnp.where(at_p[p], values[128 * p : 128 * p + 128, lane : lane + 128], 0.0)
            total = term if total is None else total + term
        return total

    def left_rows(m):
        for item in ITEMS:
            await_bytes(sixteen, sa_recv.at[item, m])
        start = (y + m) % 4 * 16

        @pl.loop(0, 16, step=8)
        def _(r):
            a = start + r
            g = ga[pl.ds(a, 8)].reshape(1024, BLOCK)
            full = lax.dot_general(
                ww[...], g, (((1,), (1,)), ((), ())), preferred_element_type=jnp.float32
            )
            for s in range(8):
                lbuf[pl.ds(pl.multiple_of((a + s) * PITCH, 8), 128)] = pick(full, 128 * s)

    odd = zlo % 2
    early, late = 1 + 2 * odd, 3 - 2 * odd
    onward = at_z(z + 17 - 2 * odd, core)

    def from_early(t):
        await_bytes(own_part, near_recv.at[early, t // 4])
        piece = share_rows(t, zhi + 4 - early)[0]
        remote(piece, piece, pass_send, near_recv.at[early, t // 4], onward).start()
        spread(t, early)

    def from_late(t):
        await_bytes(own_part, near_recv.at[late, t // 4])
        spread(t, late)

    def from_far():
        a_part, _ = share_rows(quarter, zhi + 2)
        await_bytes(a_part, z_recv)
        for m in range(1, 4):
            plane = zhi * 4 + (zlo + m) % 4
            remote(a_part, a_part, v_send, v_recv.at[m], at_z(plane, core)).start()
        spread(quarter, 2)

    def from_planes():
        for m in range(1, 4):
            t = 4 * ((zlo + 4 - m) % 4)
            await_bytes(own_part, v_recv.at[m])
            spread(t, 2)

    for way, step in ((0, 1), (1, 3)):
        x_part = xp.at[(y + 4 - step) % 4, pl.ds(32 * way, 32)]
        await_bytes(xp.at[0], x_recv.at[way])
        remote(x_part, x_part, x_send, x_recv.at[2], at_xy(x, y + step, core)).start()
    pltpu.make_async_copy(w4.at[y], wp.at[x, y], loc_sem.at[7]).wait()
    await_bytes(wp.at[0, pl.ds(0, 3)], w_recv.at[0])
    for m in range(1, 4):
        remote(wp.at[x], wp.at[x], w_send.at[1], w_recv.at[1], at_xy(x + m, y, core)).start()
    from_early(0)
    pltpu.make_async_copy(xt, xp.at[y], loc_sem.at[6]).wait()
    await_bytes(xp.at[0], x_recv.at[2])
    for p in range(4):
        for q in range(2):
            xw[128 * p + 64 * q : 128 * p + 64 * q + 64] = xp[p, :, BLOCK * q : BLOCK * q + BLOCK]
    multiply(zhi, core)
    from_early(4)
    from_late(0)
    from_far()
    from_early(8)
    from_late(4)
    from_early(12)
    from_late(8)
    from_late(12)
    hand_rows(early, 0)
    hand_rows(late, 0)
    from_planes()
    hand_rows(2, 0)
    pass_on(early)
    pass_on(late)
    pass_on(2)
    await_bytes(own_a, sa_recv.at[0, 0])
    await_bytes(own_d, sd_recv.at[0])
    multiply(zhi, 1 - core)
    await_bytes(wp.at[pl.ds(0, 3)], w_recv.at[1])
    for p in range(4):
        ww[128 * p : 128 * p + 128] = (
            wp[:, p].reshape(BLOCK, 128).astype(jnp.float32).T.astype(jnp.bfloat16)
        )
    def from_sibling(item):
        await_bytes(own_d, sd_recv.at[item])
        multiply(zhi + 4 - item, 1 - core)

    hand_over(early)
    multiply(zhi + 4 - early, core)
    hand_over(late)
    multiply(zhi + 4 - late, core)
    left_rows(0)
    hand_over(2)
    multiply(zhi + 2, core)
    from_sibling(early)
    left_rows(1)
    from_sibling(late)
    left_rows(3)
    from_sibling(2)
    left_rows(2)

    acc[...] = jnp.zeros_like(acc)

    @pl.loop(0, 64, step=16)
    def _(d):
        right = jnp.concatenate(
            [lbuf[pl.ds(q * 64 + d + s, 64, stride=PITCH)].astype(jnp.bfloat16)
             for s in range(16) for q in range(2)], axis=0)
        tiles = [rbuf[d + s] for s in range(16)]
        left = jnp.concatenate(
            [jnp.concatenate([t[:, 128 * p : 128 * p + 128] for t in tiles], axis=1) for p in range(4)],
            axis=0)
        acc[...] += jnp.dot(left, right, preferred_element_type=jnp.float32)

    part[...] = pick(acc[...], 0).T

    me = y * 4 + x
    mine = pl.ds(pl.multiple_of(8 * me, 8), 8)
    remote(part, other, red_send.at[3], red_recv.at[3], sibling).start()
    await_bytes(part, red_recv.at[3])
    both[...] = part[...] + other[...]
    for m in range(1, 16):
        xx, yy = in_plane(m)
        theirs = both.at[pl.ds(8 * (yy * 4 + xx), 8)]
        remote(theirs, rs.at[me], red_send.at[0], red_recv.at[0], at_xy(xx, yy, core)).start()
    rs[me] = both[mine]
    await_bytes(rs.at[pl.ds(0, 15)], red_recv.at[0])
    share[...] = jnp.sum(rs[...], axis=0)
    for m in range(1, 16):
        remote(share, zs.at[z], red_send.at[1], red_recv.at[1], at_z(z + m, core)).start()
    zs[z] = share[...]
    await_bytes(zs.at[pl.ds(0, 15)], red_recv.at[1])
    await_bytes(rs.at[pl.ds(0, 15)], red_send.at[0])
    await_bytes(part, red_send.at[3])
    await_bytes(zs.at[pl.ds(0, 15)], red_send.at[1])
    share[...] = jnp.sum(zs[...], axis=0)
    whole = acc.at[pl.ds(0, 128)]
    for m in range(1, 16):
        xx, yy = in_plane(m)
        remote(share, whole.at[mine], red_send.at[2], red_recv.at[2], at_xy(xx, yy, core)).start()
    whole[mine] = share[...]
    await_bytes(zs.at[pl.ds(0, 15)], red_recv.at[2])
    await_bytes(zs.at[pl.ds(0, 15)], red_send.at[2])

    schur = whole[...]
    factor = jnp.zeros((128, 128), jnp.float32)
    width = 8
    for k in range(PANELS * width):
        lo = k // width * width
        if k == lo:
            inside = (rows >= lo) & (rows < lo + width) & (lanes >= lo) & (lanes < lo + width)
            schur = jnp.where(inside, 0.5 * (schur + schur.T), schur)
        column = jnp.sum(jnp.where(lanes == k, schur, 0.0), axis=1, keepdims=True)
        pivot = jnp.sum(jnp.where(rows[:, :1] == k, column, 0.0), axis=0, keepdims=True)
        column = jnp.where(rows[:, :1] >= k, column / jnp.sqrt(pivot), 0.0)
        line = jnp.sum(jnp.where(rows == lanes, column, 0.0), axis=0, keepdims=True)
        schur = schur - column * line
        factor = jnp.where(lanes == k, column, factor)
    bound = PANELS * width
    part[...] = factor
    near = pl.ds(pl.multiple_of(row // 4 * 8, 8), 8)
    up = (8 - 2 * (row % 4)) % 8
    top = pltpu.roll(part[near], up, 0)
    part[...] = jnp.where((rows >= bound) & (lanes >= bound), schur, 0.0)
    shifted = pltpu.roll(pltpu.roll(part[near], up, 0), (128 + bound - 16 * col) % 128, 1)
    out_ref[...] = jnp.where(lanes[:8] < bound, top, shifted)[:2, : bound + 16]

    await_bytes(xp.at[pl.ds(0, 3)], x_send)
    await_bytes(wp.at[0, pl.ds(0, 3)], w_send.at[0])
    await_bytes(wp.at[pl.ds(0, 3)], w_send.at[1])
    for item in ITEMS:
        await_bytes(ga.at[pl.ds(0, 48), pl.ds(0, 16)], ya_send.at[item])
        await_bytes(ga.at[pl.ds(0, 48), pl.ds(0, 16)], xd_send.at[item])
    await_bytes(own_part, z_send)
    await_bytes(ga.at[pl.ds(0, 16), pl.ds(0, 16)], pass_send)
    await_bytes(ga.at[pl.ds(0, 12), pl.ds(0, 16)], v_send)

    @pl.when(zlo == 3)
    def _():
        await_bytes(ga.at[pl.ds(0, 32), pl.ds(0, 16)], near_send.at[0])

    @pl.when(zlo == 0)
    def _():
        await_bytes(ga.at[pl.ds(0, 32), pl.ds(0, 16)], near_send.at[1])

    for item in range(4):
        await_bytes(gd.at[:, pl.ds(0, 16)], sd_send.at[item])
    await_bytes(own_a, sa_send.at[0, 0])
    for item in ITEMS:
        for m in range(4):
            await_bytes(sixteen, sa_send.at[item, m])


def on_device(blocks, position, primal, dual_inverse):
    tile_cols = blocks.shape[0]
    rows, width = primal.shape
    per_row = tile_cols * lax.axis_size("col") // lax.axis_size("row")
    count = position.shape[0]
    vmem = pl.BlockSpec(memory_space=pltpu.VMEM)
    hbm = pl.BlockSpec(memory_space=pl.ANY)
    bf, f32 = jnp.bfloat16, jnp.float32
    dma = pltpu.SemaphoreType.DMA
    both = pl.pallas_call(
        schur_kernel,
        out_shape=jax.ShapeDtypeStruct((per_row, PANELS * 8 + tile_cols), f32),
        in_specs=[hbm, vmem, vmem, vmem],
        out_specs=vmem,
        scratch_shapes=[
            pltpu.VMEM((tile_cols, 144, BLOCK), bf),
            pltpu.VMEM((2, tile_cols * PITCH, 128), f32),
            pltpu.VMEM((4, rows, 128), bf),
            pltpu.VMEM((64, count, BLOCK), bf),
            pltpu.VMEM((64, count, BLOCK), bf),
            pltpu.VMEM((4, rows, width), bf),
            pltpu.VMEM((4, 4, rows, 128), bf),
            pltpu.VMEM((512, BLOCK), bf),
            pltpu.VMEM((512, BLOCK), bf),
            pltpu.VMEM((count, 128), f32),
            pltpu.VMEM((64, count, 512), bf),
            pltpu.VMEM((64 * PITCH, 128), f32),
            pltpu.VMEM((512, count), f32),
            pltpu.VMEM((count, count), f32),
            pltpu.VMEM((count, count), f32),
            pltpu.VMEM((count, count), f32),
            pltpu.VMEM((8, count), f32),
            pltpu.VMEM((16, 8, count), f32),
            pltpu.VMEM((16, 8, count), f32),
            dma((8,)), dma, dma((3,)), dma((2,)), dma((2,)),
            dma((2,)), dma((4, 4)), dma, dma, dma, dma, dma((4,)),
            dma((4,)), dma((4,)), dma((4, 2, 2)), dma((4, 2, 2)), dma((4,)), dma((4,)), dma((4,)),
            dma((4, 4)), dma((4,)), dma((4, 4)), dma((4,)), dma((4,)), dma((4,)),
        ],
        compiler_params=pltpu.CompilerParams(
            collective_id=0, has_side_effects=True, vmem_limit_bytes=56 << 20
        ),
        name="schur",
    )(blocks, primal, dual_inverse, position.reshape(1, count))
    return both[:, : PANELS * 8], both[:, PANELS * 8 :]


def solution(mesh):
    in_specs = (P("col", None, None), P(), P("row", "col"), P("row", "col"))
    out_specs = (P("row", None), P("row", "col"))
    return jax.shard_map(
        on_device, mesh=mesh, in_specs=in_specs, out_specs=out_specs, check_vma=False
    )
```

```python
import functools

import jax
import jax.numpy as jnp
from jax import lax
from jax.experimental import pallas as pl
from jax.experimental.pallas import tpu as pltpu
from jax.sharding import PartitionSpec as P

BLOCK = 256
PANELS = 2
MESH = pl.DeviceIdType.MESH
ITEMS = (1, 3, 2)
PITCH = 136


def remote(src, dst, send, recv, dev):
    return pltpu.make_async_remote_copy(
        src_ref=src, dst_ref=dst, send_sem=send, recv_sem=recv, device_id=dev, device_id_type=MESH
    )


def await_bytes(ref, sem):
    pltpu.make_async_copy(ref, ref, sem).wait()


def schur_kernel(
    blocks, xt, wt, pos,
    out_ref,
    raw, wide, w4, ga, gd, xp, wp, xw, ww, own_q, rbuf, lbuf, acc, part, other, both, share, rs, zs,
    loc_sem, x_send, x_recv, w_send, w_recv, near_send, near_recv, pass_send, z_send, z_recv, v_send, v_recv,
    ya_send, xd_send, ya_recv, xd_recv, yy_recv, xx_recv, cp_sem, sa_send, sd_send, sa_recv, sd_recv, red_send, red_recv,
):
    row = lax.axis_index("row")
    col = lax.axis_index("col")
    zlo, y, x = row // 16, (row // 4) % 4, row % 4
    zhi, core = col // 2, col % 2
    z = zhi * 4 + zlo
    sibling = (row, zhi * 2 + (1 - core))

    def at_z(zz, kk):
        zz = zz % 16
        return ((zz % 4) * 16 + y * 4 + x, (zz // 4) * 2 + kk)

    def at_xy(xx, yy, kk):
        return (zlo * 16 + (yy % 4) * 4 + xx % 4, zhi * 2 + kk)

    def in_plane(m):
        return (x + m % 4) % 4, (y + m // 4) % 4

    barrier = pltpu.get_barrier_semaphore()

    def greet(dev):
        pl.semaphore_signal(barrier, inc=1, device_id=dev, device_id_type=MESH)

    for m in range(1, 16):
        xx, yy = in_plane(m)
        greet(at_xy(xx, yy, core))
        greet(at_z(z + m, core))
    greet(sibling)

    def cols(h, k=None):
        start = ((h % 4) * 2 + (core if k is None else k)) * 16
        return pl.ds(pl.multiple_of(start, 16), 16)

    first = pltpu.make_async_copy(
        blocks.at[:, pl.ds(pl.multiple_of(64 * x + 16 * y, 16), 16)], raw.at[:, pl.ds(128, 16)], loc_sem.at[5])
    first.start()
    loads = [pltpu.make_async_copy(
        blocks.at[:, pl.ds(pl.multiple_of(64 * x, 64), 64)], raw.at[:, pl.ds(0, 64)], loc_sem.at[0])]
    for s in range(4):
        loads.append(pltpu.make_async_copy(
            blocks.at[:, pl.ds(pl.multiple_of(64 * s + 16 * y, 16), 16)],
            raw.at[:, pl.ds(64 + 16 * s, 16)], loc_sem.at[1 + s]))
    for load in loads:
        load.start()

    def one_row(r):
        return jnp.concatenate(
            [wide[side, pl.ds(r, 16, stride=PITCH)] for side in range(2)], axis=1
        ).astype(jnp.bfloat16)

    first.wait()
    for j in range(16):
        for side in range(2):
            wide[side, j * PITCH : j * PITCH + 16] = (
                raw[j, 128:144, 128 * side : 128 * side + 128].astype(jnp.float32))
    for r in range(16):
        line = one_row(r)
        ga[16 * y + r, cols(zhi)] = line
        gd[16 * x + r, cols(zhi)] = line

    pl.semaphore_wait(barrier, 31)

    quarter = 4 * zlo

    def share_rows(t, h):
        return (
            ga.at[pl.ds(16 * y + t, 4), cols(h)],
            gd.at[pl.ds(16 * x + t, 4), cols(h)],
        )

    own_part = share_rows(quarter, zhi)[0]

    remote(own_part, own_part, z_send, z_recv, at_z(z + 8, core)).start()

    def near(way, item, planes):
        for t in range(0, 16, 4):
            piece = share_rows(t, zhi)[0]
            for v in planes:
                remote(piece, piece, near_send.at[way], near_recv.at[item, t // 4],
                       at_z(4 * (zhi + item) + v, core)).start()

    @pl.when(zlo == 3)
    def _():
        near(0, 1, (0, 2))

    @pl.when(zlo == 0)
    def _():
        near(1, 3, (3, 1))


    for way, step in ((0, 1), (1, 3)):
        remote(xt, xp.at[y], x_send, x_recv.at[way], at_xy(x, y + step, core)).start()
    pltpu.make_async_copy(xt, xp.at[y], loc_sem.at[6]).start()

    rows = lax.broadcasted_iota(jnp.int32, (128, 128), 0)
    lanes = lax.broadcasted_iota(jnp.int32, (128, 128), 1)
    source = lax.broadcasted_iota(jnp.int32, (512, 128), 0)
    target = lax.broadcasted_iota(jnp.int32, (512, 128), 1)
    place = target // 64 * 256 + target // 16 % 4 * 64 + target % 16
    for yy in range(4):
        order = jnp.where(source == place + 16 * yy, 1.0, 0.0).astype(jnp.bfloat16)
        w4[yy] = jnp.dot(wt[...], order, preferred_element_type=jnp.float32).astype(jnp.bfloat16)
    for m in range(1, 4):
        yy = (y + m) % 4
        remote(w4.at[yy], wp.at[x, y], w_send.at[0], w_recv.at[0], at_xy(x, yy, core)).start()
    pltpu.make_async_copy(w4.at[y], wp.at[x, y], loc_sem.at[7]).start()
    for load in loads:
        load.wait()

    @pl.loop(0, 16)
    def _(j):
        start = pl.multiple_of(j * PITCH, 8)
        for side in range(2):
            wide[side, pl.ds(start, 128)] = raw[j, 0:128, 128 * side : 128 * side + 128].astype(jnp.float32)

    for m in range(1, 4):
        a_start, d_start = (y + m) % 4 * 16, (x + m) % 4 * 16

        @pl.loop(0, 16, step=8)
        def _(r):
            for s in range(8):
                ga[a_start + r + s, cols(zhi)] = one_row(a_start + r + s)
                gd[d_start + r + s, cols(zhi)] = one_row(64 + d_start + r + s)

    entry = jnp.broadcast_to(pos[...].astype(jnp.float32), (128, 128))
    own_q[...] = jnp.where(entry.T == (2 * col + lanes // 64).astype(jnp.float32), 1.0, 0.0)

    own_a, own_d = ga.at[:, cols(zhi)], gd.at[:, cols(zhi)]
    remote(own_a, own_a, sa_send.at[0, 0], sa_recv.at[0, 0], sibling).start()
    remote(own_d, own_d, sd_send.at[0], sd_recv.at[0], sibling).start()

    def multiply(h, k):
        keep = jnp.concatenate([own_q[cols(h, k)]] * 4, axis=1) > 0.5

        @pl.loop(0, 64, step=64)
        def _(d):
            g = gd[pl.ds(d, 64), cols(h, k)].reshape(1024, BLOCK)
            full = lax.dot_general(
                g, xw[...], (((1,), (1,)), ((), ())), preferred_element_type=jnp.float32
            ).reshape(64, 16, 512)
            rbuf[pl.ds(d, 64), cols(h, k)] = jnp.where(keep[None], full, 0.0).astype(jnp.bfloat16)

    def spread(t, item):
        a_part, d_part = share_rows(t, zhi + 4 - item)
        part_half = t // 8
        for way, step in ((0, 1), (1, 3)):
            remote(a_part, a_part, ya_send.at[item], ya_recv.at[item, way, part_half],
                   at_xy(x, y + step, core)).start()
            remote(a_part, d_part, xd_send.at[item], xd_recv.at[item, way, part_half],
                   at_xy(x + step, y, core)).start()
        pltpu.make_async_copy(a_part, d_part, cp_sem.at[item]).start()

    eight = ga.at[pl.ds(0, 8), pl.ds(0, 16)]

    def pass_on(item):
        for way, step in ((0, 1), (1, 3)):
            back = 4 - step
            a_part = ga.at[pl.ds((y + back) % 4 * 16 + 8 * way, 8), cols(zhi + 4 - item)]
            await_bytes(eight, ya_recv.at[item, way, way])
            remote(a_part, a_part, ya_send.at[item], yy_recv.at[item], at_xy(x, y + step, core)).start()
            d_part = gd.at[pl.ds((x + back) % 4 * 16 + 8 * way, 8), cols(zhi + 4 - item)]
            await_bytes(eight, xd_recv.at[item, way, way])
            remote(d_part, d_part, xd_send.at[item], xx_recv.at[item], at_xy(x + step, y, core)).start()

    sixteen = ga.at[pl.ds(0, 16), pl.ds(0, 16)]

    def hand_rows(item, m):
        part = ga.at[pl.ds((y + m) % 4 * 16, 16), cols(zhi + 4 - item)]
        remote(part, part, sa_send.at[item, m], sa_recv.at[item, m], sibling).start()

    def hand_over(item):
        for way in range(2):
            await_bytes(eight, ya_recv.at[item, way, 1 - way])
            hand_rows(item, 3 - 2 * way)
        await_bytes(sixteen, yy_recv.at[item])
        hand_rows(item, 2)
        for way in range(2):
            await_bytes(eight, xd_recv.at[item, way, 1 - way])
        await_bytes(sixteen, xx_recv.at[item])
        await_bytes(sixteen, cp_sem.at[item])
        part_d = gd.at[:, cols(zhi + 4 - item)]
        remote(part_d, part_d, sd_send.at[item], sd_recv.at[item], sibling).start()

    at_p = [pos[...] == 4 * zlo + p for p in range(4)]

    def pick(values, lane):
        total = None
        for p in range(4):
            term = jnp.where(at_p[p], values[128 * p : 128 * p + 128, lane : lane + 128], 0.0)
            total = term if total is None else total + term
        return total

    def left_rows(m):
        for item in ITEMS:
            await_bytes(sixteen, sa_recv.at[item, m])
        start = (y + m) % 4 * 16

        @pl.loop(0, 16, step=16)
        def _(r):
            a = start + r
            g = ga[pl.ds(a, 16)].reshape(2048, BLOCK)
            full = lax.dot_general(
                ww[...], g, (((1,), (1,)), ((), ())), preferred_element_type=jnp.float32
            )
            for s in range(16):
                lbuf[pl.ds(pl.multiple_of((a + s) * PITCH, 8), 128)] = pick(full, 128 * s)

    odd = zlo % 2
    early, late = 1 + 2 * odd, 3 - 2 * odd
    onward = at_z(z + 17 - 2 * odd, core)

    def from_early(t):
        await_bytes(own_part, near_recv.at[early, t // 4])
        piece = share_rows(t, zhi + 4 - early)[0]
        remote(piece, piece, pass_send, near_recv.at[early, t // 4], onward).start()
        spread(t, early)

    def from_late(t):
        await_bytes(own_part, near_recv.at[late, t // 4])
        spread(t, late)

    def from_far():
        a_part, _ = share_rows(quarter, zhi + 2)
        await_bytes(a_part, z_recv)
        for m in range(1, 4):
            plane = zhi * 4 + (zlo + m) % 4
            remote(a_part, a_part, v_send, v_recv.at[m], at_z(plane, core)).start()
        spread(quarter, 2)

    def from_planes():
        for m in range(1, 4):
            t = 4 * ((zlo + 4 - m) % 4)
            await_bytes(own_part, v_recv.at[m])
            spread(t, 2)

    for way, step in ((0, 1), (1, 3)):
        x_part = xp.at[(y + 4 - step) % 4, pl.ds(32 * way, 32)]
        await_bytes(xp.at[0], x_recv.at[way])
        remote(x_part, x_part, x_send, x_recv.at[2], at_xy(x, y + step, core)).start()
    pltpu.make_async_copy(w4.at[y], wp.at[x, y], loc_sem.at[7]).wait()
    await_bytes(wp.at[0, pl.ds(0, 3)], w_recv.at[0])
    for m in range(1, 4):
        remote(wp.at[x], wp.at[x], w_send.at[1], w_recv.at[1], at_xy(x + m, y, core)).start()
    from_early(0)
    pltpu.make_async_copy(xt, xp.at[y], loc_sem.at[6]).wait()
    await_bytes(xp.at[0], x_recv.at[2])
    for p in range(4):
        for q in range(2):
            xw[128 * p + 64 * q : 128 * p + 64 * q + 64] = xp[p, :, BLOCK * q : BLOCK * q + BLOCK]
    multiply(zhi, core)
    from_early(4)
    from_late(0)
    from_far()
    from_early(8)
    from_late(4)
    from_early(12)
    from_late(8)
    from_late(12)
    hand_rows(early, 0)
    hand_rows(late, 0)
    from_planes()
    hand_rows(2, 0)
    pass_on(early)
    pass_on(late)
    pass_on(2)
    await_bytes(own_a, sa_recv.at[0, 0])
    await_bytes(own_d, sd_recv.at[0])
    multiply(zhi, 1 - core)
    await_bytes(wp.at[pl.ds(0, 3)], w_recv.at[1])
    for p in range(4):
        ww[128 * p : 128 * p + 128] = (
            wp[:, p].reshape(BLOCK, 128).astype(jnp.float32).T.astype(jnp.bfloat16)
        )
    def from_sibling(item):
        await_bytes(own_d, sd_recv.at[item])
        multiply(zhi + 4 - item, 1 - core)

    hand_over(early)
    multiply(zhi + 4 - early, core)
    hand_over(late)
    multiply(zhi + 4 - late, core)
    left_rows(0)
    hand_over(2)
    multiply(zhi + 2, core)
    from_sibling(early)
    left_rows(1)
    from_sibling(late)
    left_rows(3)
    from_sibling(2)
    left_rows(2)

    acc[...] = jnp.zeros_like(acc)

    @pl.loop(0, 64, step=32)
    def _(d):
        right = jnp.concatenate(
            [lbuf[pl.ds(q * 64 + d + s, 64, stride=PITCH)].astype(jnp.bfloat16)
             for s in range(32) for q in range(2)], axis=0)
        tiles = [rbuf[d + s] for s in range(32)]
        left = jnp.concatenate(
            [jnp.concatenate([t[:, 128 * p : 128 * p + 128] for t in tiles], axis=1) for p in range(4)],
            axis=0)
        acc[...] += jnp.dot(left, right, preferred_element_type=jnp.float32)

    part[...] = pick(acc[...], 0).T

    me = y * 4 + x
    mine = pl.ds(pl.multiple_of(8 * me, 8), 8)
    remote(part, other, red_send.at[3], red_recv.at[3], sibling).start()
    await_bytes(part, red_recv.at[3])
    both[...] = part[...] + other[...]
    for m in range(1, 16):
        xx, yy = in_plane(m)
        theirs = both.at[pl.ds(8 * (yy * 4 + xx), 8)]
        remote(theirs, rs.at[me], red_send.at[0], red_recv.at[0], at_xy(xx, yy, core)).start()
    rs[me] = both[mine]
    await_bytes(rs.at[pl.ds(0, 15)], red_recv.at[0])
    share[...] = jnp.sum(rs[...], axis=0)
    for m in range(1, 16):
        remote(share, zs.at[z], red_send.at[1], red_recv.at[1], at_z(z + m, core)).start()
    zs[z] = share[...]
    await_bytes(zs.at[pl.ds(0, 15)], red_recv.at[1])
    await_bytes(rs.at[pl.ds(0, 15)], red_send.at[0])
    await_bytes(part, red_send.at[3])
    await_bytes(zs.at[pl.ds(0, 15)], red_send.at[1])
    share[...] = jnp.sum(zs[...], axis=0)
    whole = acc.at[pl.ds(0, 128)]
    for m in range(1, 16):
        xx, yy = in_plane(m)
        remote(share, whole.at[mine], red_send.at[2], red_recv.at[2], at_xy(xx, yy, core)).start()
    whole[mine] = share[...]
    await_bytes(zs.at[pl.ds(0, 15)], red_recv.at[2])
    await_bytes(zs.at[pl.ds(0, 15)], red_send.at[2])

    schur = whole[...]
    factor = jnp.zeros((128, 128), jnp.float32)
    width = 8
    for k in range(PANELS * width):
        lo = k // width * width
        if k == lo:
            inside = (rows >= lo) & (rows < lo + width) & (lanes >= lo) & (lanes < lo + width)
            schur = jnp.where(inside, 0.5 * (schur + schur.T), schur)
        column = jnp.sum(jnp.where(lanes == k, schur, 0.0), axis=1, keepdims=True)
        pivot = jnp.sum(jnp.where(rows[:, :1] == k, column, 0.0), axis=0, keepdims=True)
        column = jnp.where(rows[:, :1] >= k, column / jnp.sqrt(pivot), 0.0)
        line = jnp.sum(jnp.where(rows == lanes, column, 0.0), axis=0, keepdims=True)
        schur = schur - column * line
        factor = jnp.where(lanes == k, column, factor)
    bound = PANELS * width
    part[...] = factor
    near = pl.ds(pl.multiple_of(row // 4 * 8, 8), 8)
    up = (8 - 2 * (row % 4)) % 8
    top = pltpu.roll(part[near], up, 0)
    part[...] = jnp.where((rows >= bound) & (lanes >= bound), schur, 0.0)
    shifted = pltpu.roll(pltpu.roll(part[near], up, 0), (128 + bound - 16 * col) % 128, 1)
    out_ref[...] = jnp.where(lanes[:8] < bound, top, shifted)[:2, : bound + 16]

    await_bytes(xp.at[pl.ds(0, 3)], x_send)
    await_bytes(wp.at[0, pl.ds(0, 3)], w_send.at[0])
    await_bytes(wp.at[pl.ds(0, 3)], w_send.at[1])
    for item in ITEMS:
        await_bytes(ga.at[pl.ds(0, 48), pl.ds(0, 16)], ya_send.at[item])
        await_bytes(ga.at[pl.ds(0, 48), pl.ds(0, 16)], xd_send.at[item])
    await_bytes(own_part, z_send)
    await_bytes(ga.at[pl.ds(0, 16), pl.ds(0, 16)], pass_send)
    await_bytes(ga.at[pl.ds(0, 12), pl.ds(0, 16)], v_send)

    @pl.when(zlo == 3)
    def _():
        await_bytes(ga.at[pl.ds(0, 32), pl.ds(0, 16)], near_send.at[0])

    @pl.when(zlo == 0)
    def _():
        await_bytes(ga.at[pl.ds(0, 32), pl.ds(0, 16)], near_send.at[1])

    for item in range(4):
        await_bytes(gd.at[:, pl.ds(0, 16)], sd_send.at[item])
    await_bytes(own_a, sa_send.at[0, 0])
    for item in ITEMS:
        for m in range(4):
            await_bytes(sixteen, sa_send.at[item, m])


def on_device(blocks, position, primal, dual_inverse):
    tile_cols = blocks.shape[0]
    rows, width = primal.shape
    per_row = tile_cols * lax.axis_size("col") // lax.axis_size("row")
    count = position.shape[0]
    vmem = pl.BlockSpec(memory_space=pltpu.VMEM)
    hbm = pl.BlockSpec(memory_space=pl.ANY)
    bf, f32 = jnp.bfloat16, jnp.float32
    dma = pltpu.SemaphoreType.DMA
    both = pl.pallas_call(
        schur_kernel,
        out_shape=jax.ShapeDtypeStruct((per_row, PANELS * 8 + tile_cols), f32),
        in_specs=[hbm, vmem, vmem, vmem],
        out_specs=vmem,
        scratch_shapes=[
            pltpu.VMEM((tile_cols, 144, BLOCK), bf),
            pltpu.VMEM((2, tile_cols * PITCH, 128), f32),
            pltpu.VMEM((4, rows, 128), bf),
            pltpu.VMEM((64, count, BLOCK), bf),
            pltpu.VMEM((64, count, BLOCK), bf),
            pltpu.VMEM((4, rows, width), bf),
            pltpu.VMEM((4, 4, rows, 128), bf),
            pltpu.VMEM((512, BLOCK), bf),
            pltpu.VMEM((512, BLOCK), bf),
            pltpu.VMEM((count, 128), f32),
            pltpu.VMEM((64, count, 512), bf),
            pltpu.VMEM((64 * PITCH, 128), f32),
            pltpu.VMEM((512, count), f32),
            pltpu.VMEM((count, count), f32),
            pltpu.VMEM((count, count), f32),
            pltpu.VMEM((count, count), f32),
            pltpu.VMEM((8, count), f32),
            pltpu.VMEM((16, 8, count), f32),
            pltpu.VMEM((16, 8, count), f32),
            dma((8,)), dma, dma((3,)), dma((2,)), dma((2,)),
            dma((2,)), dma((4, 4)), dma, dma, dma, dma, dma((4,)),
            dma((4,)), dma((4,)), dma((4, 2, 2)), dma((4, 2, 2)), dma((4,)), dma((4,)), dma((4,)),
            dma((4, 4)), dma((4,)), dma((4, 4)), dma((4,)), dma((4,)), dma((4,)),
        ],
        compiler_params=pltpu.CompilerParams(
            collective_id=0, has_side_effects=True, vmem_limit_bytes=56 << 20
        ),
        name="schur",
    )(blocks, primal, dual_inverse, position.reshape(1, count))
    return both[:, : PANELS * 8], both[:, PANELS * 8 :]


def solution(mesh):
    in_specs = (P("col", None, None), P(), P("row", "col"), P("row", "col"))
    out_specs = (P("row", None), P("row", "col"))
    return jax.shard_map(
        on_device, mesh=mesh, in_specs=in_specs, out_specs=out_specs, check_vma=False
    )
```
